512 devices in a mesh: kv: 32 (over z, core), tp: 16 (over y, x).
Axes of the slice: x: 4, y: 4, z: 16, core: 2. Of those that a mesh axis runs over, the one named last changes fastest.
Arguments:
- queries: bfloat16 [4, 8192], replicated, may hold values from -7 to 7
- res_cache: bfloat16 [16384, 2, 8, 512], P(('kv', 'tp')), may hold values from -12.5 to 12.5
- res_count: int32 [512, 4], P(('kv', 'tp')), may hold values from 1 to 16, 32 in all within a row
- move_cache: bfloat16 [16384, 2, 8, 512], P(('kv', 'tp')), may hold values from -12.5 to 12.5
- move_request: int32 [16384], P(('kv', 'tp')), may hold values from 0 to 3
- move_owner: int32 [16384, 1], P(('kv', 'tp')), may hold values from 0 to 31; in each aligned block of 32 rows (0 to 31, 32 to 63, ...) at most 2 rows name the same one
- out_weight: bfloat16 [8192, 16384], P('kv', 'tp'), may hold values from -0.0625 to 0.0625
Outputs:
- mixed: bfloat16 [4, 16384], P(None, 'tp')
- landed_pages: bfloat16 [32768, 2, 8, 512], P(('kv', 'tp'))
- landed_request: int32 [32768], P(('kv', 'tp'))
The draws below stay inside these ranges and needn't reach their ends.
Inputs may be any that keep to these rules, and one draw needn't show every extreme that they name: `res_count`: each row sums to 32: every resident slot is used, slots filled in request order, every request on every block. `move_owner`: at most 2 of the 32 outgoing pages of one device name one owner.
All inputs are finite; a program needn't handle non-finite values.
Results may differ from the reference program's by a relative error of at most 0.01.
Values may be sent and summed in bfloat16 or wider, within the bound.
No kernel may reach another device: no remote copies, remote signals or barrier semaphores. Data moves between devices by JAX's collectives and lax.ppermute only.
A program may use at most 192 MiB of HBM per device.

```python
import math
import jax
import jax.numpy as jnp
import numpy as np
from jax import lax

D = 16384
HQ = 64
KVH = 4
HD = 128
GROUP = 16
B = 4
PAGE = 8
CAP = 2
RES = 32
MOVE = 32
SLOTS_ALL = 16384
MOVE_ALL = 16384
LAND_ALL = 32768
N_KV = 32
N_TP = 16


def page_values(key, page_count):
    page_shape = (page_count, 2, PAGE, KVH * HD)
    raw_values = jnp.clip(jax.random.normal(key, page_shape, jnp.float32), -3.0, 3.0)
    key_part = jnp.where(jnp.arange(2) == 0, 2.5, 1.0).astype(jnp.float32)[None, :, None, None]
    return raw_values * key_part


def draw_queries(key, part):
    key = jax.random.fold_in(key, 1)
    query_shape = (B, KVH, GROUP, HD)
    drawn = jnp.clip(jax.random.normal(key, query_shape, jnp.float32), -4.0, 4.0)
    return drawn.reshape(B, HQ * HD).astype(jnp.bfloat16)


def draw_res_cache(key, part):
    key = jax.random.fold_in(key, 2)
    drawn = page_values(key, SLOTS_ALL)
    return drawn.astype(jnp.bfloat16)


def draw_move_cache(key, part):
    key = jax.random.fold_in(key, 3)
    return page_values(key, MOVE_ALL).astype(jnp.bfloat16)


def with_ends(values, stream_key, smallest, largest):
    longest = values.shape.index(max(values.shape))
    spots = []
    for shift in (0, 1):
        where = [jax.random.randint(jax.random.fold_in(stream_key, axis), (), 0, length) for axis, length in enumerate(values.shape)]
        where[longest] = (where[longest] + shift) % values.shape[longest]
        spots.append(tuple(where))
    return values.at[spots[0]].set(smallest).at[spots[1]].set(largest)


def shard_levels(rng, extent, cuts, low, top_value):
    def one(dim, shards_of):
        draws = jax.random.uniform(jax.random.fold_in(jax.random.fold_in(rng, 6), dim), (shards_of,), jnp.float32, low / len(cuts), top_value / len(cuts))
        return jnp.repeat(jnp.exp(draws), extent[dim] // shards_of).reshape((-1,) + (1,) * (len(extent) - dim - 1))

    level = one(*cuts[0])
    for cut in cuts[1:]:
        level = level * one(*cut)
    return level


def profile(amount, total, limit, slope):
    weights = [(1 << 20) // math.isqrt(rank ** slope) + 1 for rank in range(2, amount + 1)]
    spare, counts = total - limit - (amount - 1), [1] * (amount - 1)
    while spare > 0:
        free = [i for i in range(amount - 1) if counts[i] < limit]
        mass, left = sum([weights[i] for i in free]), spare
        for i in free:
            addition = min(limit - counts[i], max(1, left * weights[i] // mass), spare)
            counts[i] = counts[i] + addition
            spare = spare - addition
    return np.array([limit] + counts)


def ragged_sizes(stream_key, amount, total, bound, skew):
    if amount == 2:
        one = jax.random.randint(stream_key, (), max(1, total - bound), min(bound, total - 1) + 1)
        return jnp.stack([one, total - one])
    lengths = jnp.asarray(profile(amount, total, bound, skew), jnp.int32)
    couples = (amount - 1) // 2
    source_of, taker = lengths[1:1 + 2 * couples:2], lengths[2:2 + 2 * couples:2]
    margin = jnp.minimum(source_of - 1, bound - taker)
    shifted = jax.random.randint(jax.random.fold_in(stream_key, 1), (couples,), 0, 1 << 20) % (margin + 1)
    lengths = lengths.at[1:1 + 2 * couples:2].set(source_of - shifted).at[2:2 + 2 * couples:2].set(taker + shifted)
    return lengths[jax.random.permutation(jax.random.fold_in(stream_key, 2), amount)]


def shared_out(key, own, number, rows, number_of, top, reach, skew):
    ranking = jax.random.permutation(key, number_of)
    crowded, ordinary = portions_of(number_of, rows * top, reach, skew, True), portions_of(number_of, rows * top, reach, skew, False)
    places = jnp.arange(number_of)

    def named(sizes, rotation):
        used = int((sizes > 0).sum())
        fixed = max(1, used // 4)
        moved = fixed + (places - fixed + rotation * (used - fixed)) % max(1, number_of - fixed)
        return jnp.zeros((number_of,), jnp.int32).at[ranking[jnp.where(places < fixed, places, moved)]].set(jnp.asarray(sizes, jnp.int32))

    sizes = jnp.where(number % 4 == 0, named(crowded, number // 4), named(ordinary, number - number // 4 - 1))
    mixed = jax.random.permutation(jax.random.fold_in(own, 3), number_of)
    giver, sink = mixed[0:number_of // 2 * 2:2], mixed[1:number_of // 2 * 2:2]
    slack = jnp.minimum(sizes[giver] - 1, reach - sizes[sink]) // 2
    slack = jnp.where((giver == ranking[0]) | (sink == ranking[0]) | (sizes[sink] == 0), 0, jnp.maximum(slack, 0))
    moved = jax.random.randint(jax.random.fold_in(own, 4), (number_of // 2,), 0, 1 << 20) % (slack + 1)
    sizes = sizes.at[giver].add(-moved).at[sink].add(moved)
    members = jnp.searchsorted(jnp.cumsum(sizes), jnp.arange(rows * top), side="right").astype(jnp.int32)
    grid = members.reshape(top, rows).T
    grid = grid[jax.random.permutation(jax.random.fold_in(own, 1), rows)]
    rotation = jax.random.randint(jax.random.fold_in(own, 2), (rows, 1), 0, top)
    return jnp.take_along_axis(grid, (jnp.arange(top)[None, :] + rotation) % top, axis=1)


def portions_of(number_of, total, most, lean, full):
    weights = [(1 << 20) // math.isqrt(standing ** lean) + 1 for standing in range(1, number_of + 1)]
    largest = most if full else min(most, max(-(-total // number_of), total * weights[0] // sum(weights)))
    least = 1 if total - largest >= number_of - 1 else 0
    holding, spare = [largest] + [least] * (number_of - 1), total - largest - least * (number_of - 1)
    while spare > 0:
        candidates = [i for i in range(1, number_of) if holding[i] < largest] or [i for i in range(1, number_of) if holding[i] < most]
        pool, left = sum([weights[i] for i in candidates]), spare
        for i in candidates:
            more = min(most - holding[i], max(1, left * weights[i] // pool), spare)
            holding[i] = holding[i] + more
            spare = spare - more
    return np.array(holding)


def centred(rng, extent, deviation, most, pieces=(), kind=jnp.bfloat16):
    values = deviation * jax.random.normal(rng, extent, jnp.float32)
    if pieces:
        values = values * shard_levels(rng, extent, pieces, -0.22, 0.18)
    return jnp.clip(values, -most, most).astype(kind)


def setup_inputs(seed: int = 0) -> dict:
    keys = jax.random.split(jax.random.key(seed), 8)
    queries = draw_queries(jax.random.fold_in(keys[7], 71), 0)
    res_cache = draw_res_cache(jax.random.fold_in(keys[7], 71), 0)
    res_count = jax.vmap(lambda own: ragged_sizes(own, B, RES, min(RES // 2, RES - B + 1), 2))(jax.random.split(keys[2], (N_KV * N_TP))).reshape((N_KV * N_TP, B)).astype(jnp.int32)
    move_cache = draw_move_cache(jax.random.fold_in(keys[7], 71), 0)
    move_request = with_ends(jax.random.randint(keys[4], (MOVE_ALL,), 0, B), jax.random.fold_in(keys[4], 1), 0, B - 1).astype(jnp.int32)
    move_owner_keys = jax.random.split(jax.random.fold_in(keys[5], 1), MOVE_ALL // MOVE)
    move_owner_turns = jax.random.permutation(jax.random.fold_in(keys[5], 3), MOVE_ALL // MOVE)
    move_owner = jax.vmap(lambda own, number: shared_out(jax.random.fold_in(keys[5], 2), own, number, MOVE, N_KV, 1, CAP, 2))(move_owner_keys, move_owner_turns).reshape((MOVE_ALL, 1))
    out_weight = centred(keys[6], (HQ * HD, D), (HQ * HD) ** -0.5, 0.0625, ((0, 32), (1, 16)))
    return {"queries": queries, "res_cache": res_cache, "res_count": res_count, "move_cache": move_cache, "move_request": move_request, "move_owner": move_owner, "out_weight": out_weight}


NEG = -1e+30

def absorb(running, pages, page_request, query_heads, score_scale):
    peak_old, weight_old, summed_old = running
    page_count = pages.shape[0]
    key_rows = pages[:, 0].astype(jnp.float32).reshape(page_count * PAGE, KVH, HD)
    value_rows = pages[:, 1].astype(jnp.float32).reshape(page_count * PAGE, KVH, HD)
    token_request = jnp.repeat(page_request.astype(jnp.int32), PAGE)
    wanted = (token_request[None, :] == jnp.arange(B, dtype=jnp.int32)[:, None])[:, None, None, :]
    scores = jnp.einsum('bgih,tgh->bgit', query_heads, key_rows) * score_scale
    scores = jnp.where(wanted, scores, NEG)
    peak_new = jnp.maximum(peak_old, lax.optimization_barrier(jnp.max(scores, axis=-1)))
    weights = jnp.where(wanted, jnp.exp(scores - peak_new[..., None]), 0.0).astype(jnp.bfloat16)
    weights = lax.optimization_barrier(weights).astype(jnp.float32)
    factor = jnp.exp(peak_old - peak_new)
    weight_new = weight_old * factor + lax.optimization_barrier(jnp.sum(weights, axis=-1))
    summed_new = summed_old * factor[..., None] + jnp.einsum('bgit,tgh->bgih', weights, value_rows)
    return (peak_new, weight_new, summed_new)

def reference(queries, res_cache, res_count, move_cache, move_request, move_owner, out_weight):
    devices_all = N_KV * N_TP
    query_heads = queries.astype(jnp.float32).reshape(B, KVH, GROUP, HD)
    score_scale = 1.0 / math.sqrt(HD)
    slot_ends = jnp.cumsum(res_count, axis=1)
    slot_index = jnp.arange(RES, dtype=jnp.int32)
    slot_request = lax.optimization_barrier(jnp.sum((slot_index[None, :, None] >= slot_ends[:, None, :]).astype(jnp.int32), axis=2)).astype(jnp.int32)
    initial = (jnp.full((B, KVH, GROUP), NEG, jnp.float32), jnp.zeros((B, KVH, GROUP), jnp.float32), jnp.zeros((B, KVH, GROUP, HD), jnp.float32))

    def absorb_block(running, page_block):
        return (absorb(running, page_block[0], page_block[1], query_heads, score_scale), None)
    running, _ = lax.scan(absorb_block, initial, (res_cache.reshape(devices_all, RES, 2, PAGE, KVH * HD), slot_request))
    running, _ = lax.scan(absorb_block, running, (move_cache.reshape(devices_all, MOVE, 2, PAGE, KVH * HD), move_request.reshape(devices_all, MOVE)))
    weight_sum, summed = (running[1], running[2])
    attended = (summed / weight_sum[..., None]).reshape(B, HQ * HD).astype(jnp.bfloat16)
    mixed = jnp.dot(attended, out_weight, preferred_element_type=jnp.float32).astype(jnp.bfloat16)
    owners = move_owner.reshape(devices_all, MOVE).astype(jnp.int32)
    places = (owners[:, :, None] == jnp.arange(N_KV, dtype=jnp.int32)[None, None, :]).astype(jnp.int32)
    page_rank = (lax.optimization_barrier(jnp.sum(jnp.cumsum(places, axis=1) * places, axis=2)) - 1).astype(jnp.int32)
    device = jnp.arange(devices_all, dtype=jnp.int32)[:, None]
    source = device // N_TP
    column = device % N_TP
    row_index = (((owners * N_TP + column) * N_KV + source) * CAP + page_rank).reshape(-1).astype(jnp.int32)
    landed_pages = jnp.zeros((LAND_ALL, 2, PAGE, KVH * HD), jnp.bfloat16).at[row_index].set(move_cache)
    landed_request = jnp.full((LAND_ALL,), -1, jnp.int32).at[row_index].set(move_request.astype(jnp.int32))
    return (mixed, landed_pages, landed_request)
```

```python
import math

import jax
import jax.numpy as jnp
from jax import lax
from jax.experimental import pallas as pl
from jax.experimental.pallas import tpu as pltpu
from jax.sharding import PartitionSpec as P

HQ = 64
KVH = 4
HD = 128
GROUP = 16
B = 4
PAGE = 8
CAP = 2
NEG = -1e30

VMEM = pl.BlockSpec(memory_space=pltpu.VMEM)
SMEM = pl.BlockSpec(memory_space=pltpu.SMEM)
F32 = jnp.float32
BF16 = jnp.bfloat16


def iota(shape, dim):
    return lax.broadcasted_iota(jnp.int32, shape, dim)


def round_up(x):
    return (x + jnp.abs(x) * 2.0**-7).astype(BF16).astype(F32)


def token_rows(ref, part):
    pages = ref[:, part].astype(F32)
    return pages.reshape(pages.shape[0] * PAGE, KVH * HD).astype(BF16)


def attend_kernel(q_ref, res_ref, move_ref, count_ref, request_ref, owner_ref, request_row_ref, out_ref):
    rows = GROUP * B
    n_res, n_move = res_ref.shape[0], move_ref.shape[0]
    page = iota((8, n_res * PAGE), 1) // PAGE
    end = jnp.int32(0)
    res_request = jnp.zeros_like(page)
    for b in range(B - 1):
        end = end + count_ref[0, b]
        res_request = res_request + (page >= end).astype(jnp.int32)
    page = iota((8, n_move * PAGE), 1) // PAGE
    move_request = jnp.zeros_like(page)
    for p in range(n_move):
        move_request = jnp.where(page == p, request_ref[p], move_request)
    token_request = jnp.concatenate([res_request, move_request], axis=1)
    wanted = iota((8, token_request.shape[1]), 0) % B == token_request
    wanted = jnp.concatenate([wanted.astype(F32)] * (rows // 8), axis=0) > 0.5

    keys = jnp.concatenate([token_rows(res_ref, 0), token_rows(move_ref, 0)], axis=0)
    values = jnp.concatenate([token_rows(res_ref, 1), token_rows(move_ref, 1)], axis=0)
    q = q_ref[...].astype(F32)

    owner = owner_ref[...]
    column = jnp.sum(
        jnp.where(iota((n_move, n_move), 0) == iota((n_move, n_move), 1), owner, 0), axis=1, keepdims=True
    )
    before = (column == owner) & (iota((n_move, n_move), 0) < iota((n_move, n_move), 1))
    rank = jnp.sum(before.astype(jnp.int32), axis=0, keepdims=True)
    all_rows = out_ref.shape[0] * 8
    named = iota((all_rows, n_move), 0) // 8 == owner
    marks = request_row_ref[...] + 1
    slot_ids = [
        (jnp.sum(jnp.where(named & (rank == r), marks, 0), axis=1, keepdims=True) - 1).astype(F32)
        for r in range(CAP)
    ]

    lane = iota((rows, HD), 1)
    per = rows // 8
    for g in range(KVH):
        heads = [q[:, (g * GROUP + i) * HD : (g * GROUP + i + 1) * HD] for i in range(GROUP)]
        q_rows = jnp.concatenate(heads, axis=0).astype(BF16)
        scores = lax.dot_general(
            q_rows, keys[:, g * HD : (g + 1) * HD], (((1,), (1,)), ((), ())), preferred_element_type=F32
        ) * (1.0 / math.sqrt(HD))
        scores = jnp.where(wanted, scores, NEG)
        shift = round_up(jnp.max(scores, axis=1, keepdims=True))
        weights = jnp.where(wanted, jnp.exp(scores - shift), 0.0).astype(BF16)
        weight_sum = jnp.sum(weights.astype(F32), axis=1, keepdims=True)
        summed = jnp.dot(weights, values[:, g * HD : (g + 1) * HD], preferred_element_type=F32)
        own = slice(g * rows, (g + 1) * rows)
        extra = jnp.where(lane == 0, shift, jnp.where(lane == 1, weight_sum, 0.0))
        for r in range(CAP):
            extra = jnp.where(lane == 2 + r, slot_ids[r][own], extra)
        both = jnp.concatenate([summed.reshape(per, 8, HD), extra.reshape(per, 8, HD)], axis=1)
        out_ref[g * per : (g + 1) * per] = both.astype(BF16)


def pack_kernel(move_ref, owner_ref, out_ref, used_ref):
    n_move, slots = move_ref.shape[0], out_ref.shape[0]
    out_ref[...] = jnp.zeros(out_ref.shape, out_ref.dtype)
    for o in range(slots // CAP):
        used_ref[o] = 0

    def place(p, carry):
        owner = owner_ref[p]
        rank = used_ref[owner]
        used_ref[owner] = rank + 1
        out_ref[owner * CAP + rank] = move_ref[p]
        return carry

    lax.fori_loop(0, n_move, place, 0)


def combined(parts):
    shifts, sums, values = parts[:, 8:, 0:1], parts[:, 8:, 1:2], parts[:, :8, :]
    shift = jnp.max(shifts, axis=0)
    factor = jnp.exp(shifts - shift[None])
    return shift, jnp.sum(sums * factor, axis=0), jnp.sum(values * factor, axis=0)


def column_kernel(parts_ref, out_ref, ids_ref):
    parts = parts_ref[...].astype(F32)
    shift, weight_sum, values = combined(parts)
    lane = iota((8, HD), 1)
    extra = jnp.where(lane == 0, shift, jnp.where(lane == 1, weight_sum, 0.0))
    out_ref[...] = jnp.concatenate([values, extra], axis=0)
    n = parts.shape[0]
    source, place = iota((n, n * CAP), 0), iota((n, n * CAP), 1)
    ids = parts[:, 8, :]
    ids = jnp.where(place % CAP == 0, ids[:, 2:3], ids[:, 3:4])
    ids_ref[...] = jnp.sum(jnp.where(source == place // CAP, ids, 0.0), axis=0, keepdims=True).astype(jnp.int32)


def project_kernel(parts_ref, weight_ref, out_ref):
    _, weight_sum, values = combined(parts_ref[...])
    attended = (values / weight_sum).astype(BF16)
    total = jnp.zeros((8, weight_ref.shape[1]), F32)
    upper = jnp.dot(attended, weight_ref[:HD], preferred_element_type=F32)
    lower = jnp.dot(attended, weight_ref[HD:], preferred_element_type=F32)
    out_ref[...] = (upper[:B] + lower[B:]).astype(out_ref.dtype)


def add_kernel(parts_ref, out_ref):
    out_ref[...] = jnp.sum(parts_ref[...].astype(F32), axis=0).astype(out_ref.dtype)


def local(queries, res_cache, res_count, move_cache, move_request, move_owner, out_weight):
    kv_size = lax.axis_size("kv")
    owners = move_owner.reshape(-1)
    parts = pl.pallas_call(
        attend_kernel,
        out_shape=jax.ShapeDtypeStruct((kv_size, 16, HD), BF16),
        in_specs=[VMEM, VMEM, VMEM, SMEM, SMEM, VMEM, VMEM],
        out_specs=VMEM,
        name="attend",
    )(queries, res_cache, move_cache, res_count, move_request, owners[None, :], move_request[None, :])
    outgoing = pl.pallas_call(
        pack_kernel,
        out_shape=jax.ShapeDtypeStruct((kv_size * CAP,) + move_cache.shape[1:], BF16),
        in_specs=[VMEM, SMEM],
        out_specs=VMEM,
        scratch_shapes=[pltpu.SMEM((kv_size,), jnp.int32)],
        name="pack",
    )(move_cache, owners)
    parts = lax.all_to_all(parts, "kv", split_axis=0, concat_axis=0, tiled=True)
    landed = lax.all_to_all(outgoing, "kv", split_axis=0, concat_axis=0, tiled=True)
    part, landed_ids = pl.pallas_call(
        column_kernel,
        out_shape=(
            jax.ShapeDtypeStruct((16, HD), F32),
            jax.ShapeDtypeStruct((1, kv_size * CAP), jnp.int32),
        ),
        in_specs=[VMEM],
        out_specs=(VMEM, VMEM),
        name="column",
    )(parts)
    columns = lax.all_gather(part, "tp")
    partial_out = pl.pallas_call(
        project_kernel,
        out_shape=jax.ShapeDtypeStruct((B, out_weight.shape[1]), BF16),
        in_specs=[VMEM, VMEM],
        out_specs=VMEM,
        name="project",
    )(columns, out_weight)
    partials = lax.all_gather(partial_out, "kv")
    mixed = pl.pallas_call(
        add_kernel,
        out_shape=jax.ShapeDtypeStruct((B, out_weight.shape[1]), BF16),
        in_specs=[VMEM],
        out_specs=VMEM,
        name="add",
    )(partials)
    return (mixed, landed, landed_ids.reshape(-1))


def solution(mesh):
    placed = (
        P(),
        P(("kv", "tp"), None, None, None),
        P(("kv", "tp"), None),
        P(("kv", "tp"), None, None, None),
        P(("kv", "tp")),
        P(("kv", "tp"), None),
        P("kv", "tp"),
    )
    return jax.shard_map(
        local,
        mesh=mesh,
        in_specs=placed,
        out_specs=(P(None, "tp"), P(("kv", "tp"), None, None, None), P(("kv", "tp"))),
        check_vma=False,
    )
```

```python
import math

import jax
import jax.numpy as jnp
from jax import lax
from jax.experimental import pallas as pl
from jax.experimental.pallas import tpu as pltpu
from jax.sharding import PartitionSpec as P

HQ = 64
KVH = 4
HD = 128
GROUP = 16
B = 4
PAGE = 8
CAP = 2
CHIPS = 16
NEG = -1e30

VMEM = pl.BlockSpec(memory_space=pltpu.VMEM)
SMEM = pl.BlockSpec(memory_space=pltpu.SMEM)
F32 = jnp.float32
BF16 = jnp.bfloat16


def iota(shape, dim):
    return lax.broadcasted_iota(jnp.int32, shape, dim)


def round_up(x):
    return (x + jnp.abs(x) * 2.0**-7).astype(BF16).astype(F32)


def token_rows(ref, part):
    pages = ref[:, part].astype(F32)
    return pages.reshape(pages.shape[0] * PAGE, KVH * HD).astype(BF16)


def attend_kernel(q_ref, res_ref, move_ref, count_ref, request_ref, owner_ref, request_row_ref, out_ref):
    rows = GROUP * B
    n_res, n_move = res_ref.shape[0], move_ref.shape[0]
    page = iota((8, n_res * PAGE), 1) // PAGE
    end = jnp.int32(0)
    res_request = jnp.zeros_like(page)
    for b in range(B - 1):
        end = end + count_ref[0, b]
        res_request = res_request + (page >= end).astype(jnp.int32)
    page = iota((8, n_move * PAGE), 1) // PAGE
    move_request = jnp.zeros_like(page)
    for p in range(n_move):
        move_request = jnp.where(page == p, request_ref[p], move_request)
    token_request = jnp.concatenate([res_request, move_request], axis=1)
    wanted = iota((8, token_request.shape[1]), 0) % B == token_request
    wanted = jnp.concatenate([wanted.astype(F32)] * (rows // 8), axis=0) > 0.5

    keys = jnp.concatenate([token_rows(res_ref, 0), token_rows(move_ref, 0)], axis=0)
    values = jnp.concatenate([token_rows(res_ref, 1), token_rows(move_ref, 1)], axis=0)
    q = q_ref[...].astype(F32)

    owner = owner_ref[...]
    column = jnp.sum(
        jnp.where(iota((n_move, n_move), 0) == iota((n_move, n_move), 1), owner, 0), axis=1, keepdims=True
    )
    before = (column == owner) & (iota((n_move, n_move), 0) < iota((n_move, n_move), 1))
    rank = jnp.sum(before.astype(jnp.int32), axis=0, keepdims=True)
    all_rows = out_ref.shape[0] * 8
    named = iota((all_rows, n_move), 0) // 8 == owner
    marks = request_row_ref[...] + 1
    slot_ids = [
        (jnp.sum(jnp.where(named & (rank == r), marks, 0), axis=1, keepdims=True) - 1).astype(F32)
        for r in range(CAP)
    ]

    lane = iota((rows, HD), 1)
    per = rows // 8
    for g in range(KVH):
        heads = [q[:, (g * GROUP + i) * HD : (g * GROUP + i + 1) * HD] for i in range(GROUP)]
        q_rows = jnp.concatenate(heads, axis=0).astype(BF16)
        scores = lax.dot_general(
            q_rows, keys[:, g * HD : (g + 1) * HD], (((1,), (1,)), ((), ())), preferred_element_type=F32
        ) * (1.0 / math.sqrt(HD))
        scores = jnp.where(wanted, scores, NEG)
        shift = round_up(jnp.max(scores, axis=1, keepdims=True))
        weights = jnp.where(wanted, jnp.exp(scores - shift), 0.0).astype(BF16)
        weight_sum = jnp.sum(weights.astype(F32), axis=1, keepdims=True)
        summed = jnp.dot(weights, values[:, g * HD : (g + 1) * HD], preferred_element_type=F32)
        own = slice(g * rows, (g + 1) * rows)
        extra = jnp.where(lane == 0, shift, jnp.where(lane == 1, weight_sum, 0.0))
        for r in range(CAP):
            extra = jnp.where(lane == 2 + r, slot_ids[r][own], extra)
        both = jnp.concatenate([summed.reshape(per, 8, HD), extra.reshape(per, 8, HD)], axis=1)
        out_ref[g * per : (g + 1) * per] = both.astype(BF16)


def pack_kernel(move_ref, owner_ref, own_ref, other_ref, used_ref):
    own_ref[...] = jnp.zeros(own_ref.shape, own_ref.dtype)
    other_ref[...] = jnp.zeros(other_ref.shape, other_ref.dtype)
    for o in range(used_ref.shape[0]):
        used_ref[o] = 0
    me = lax.axis_index("kv")
    chip, core = me // 2, me % 2

    def place(p, carry):
        owner = owner_ref[p]
        rank = used_ref[owner]
        used_ref[owner] = rank + 1
        slot = ((owner // 2 - chip) & (CHIPS - 1)) * CAP + rank

        @pl.when(owner % 2 == core)
        def _():
            own_ref[slot] = move_ref[p]

        @pl.when(owner % 2 != core)
        def _():
            other_ref[slot] = move_ref[p]

        return carry

    lax.fori_loop(0, move_ref.shape[0], place, 0)


UP = (4, 5, 6, 7)
DOWN = (12, 11, 10, 9)
NEAR = (0, 1, 2, 3, 15, 14, 13)
CHUNK = 2 * CAP


def merge_kernel(own_ref, got_ref, up_ref, down_ref, far_ref, near_ref):
    core = lax.axis_index("kv") % 2
    for ref, distances in ((up_ref, UP), (down_ref, DOWN), (far_ref, (8,)), (near_ref, NEAR)):
        for n, distance in enumerate(distances):
            ref[pl.ds(n * CHUNK + core * CAP, CAP)] = own_ref[distance * CAP : (distance + 1) * CAP]
            ref[pl.ds(n * CHUNK + (1 - core) * CAP, CAP)] = got_ref[distance * CAP : (distance + 1) * CAP]


def forward_kernel(near_ref, up_ref, down_ref, after_ref, *out_refs):
    del after_ref
    for n in range(3):
        own, came = slice((n + 1) * CHUNK, (n + 2) * CHUNK), slice((n + 4) * CHUNK, (n + 5) * CHUNK)
        out_refs[2 * n][:CHUNK] = near_ref[own]
        out_refs[2 * n][CHUNK:] = up_ref[own]
        out_refs[2 * n + 1][:CHUNK] = near_ref[came]
        out_refs[2 * n + 1][CHUNK:] = down_ref[own]


def land_kernel(near_ref, up_ref, down_ref, far_ref, *refs):
    out_ref = refs[-1]
    chip = lax.axis_index("kv") // 2

    def put(back, pages):
        source = (chip + back) & (CHIPS - 1)
        out_ref[pl.ds(source * CHUNK, CHUNK)] = pages

    put(0, near_ref[:CHUNK])
    put(-4, up_ref[:CHUNK])
    put(4, down_ref[:CHUNK])
    put(8, far_ref[...])
    for n in range(3):
        put(-n - 1, refs[2 * n][:CHUNK])
        put(-n - 5, refs[2 * n][CHUNK:])
        put(n + 1, refs[2 * n + 1][:CHUNK])
        put(n + 5, refs[2 * n + 1][CHUNK:])


def combined(parts):
    shifts, sums, values = parts[:, 8:, 0:1], parts[:, 8:, 1:2], parts[:, :8, :]
    shift = jnp.max(shifts, axis=0)
    factor = jnp.exp(shifts - shift[None])
    return shift, jnp.sum(sums * factor, axis=0), jnp.sum(values * factor, axis=0)


def column_kernel(parts_ref, out_ref, ids_ref):
    parts = parts_ref[...].astype(F32)
    shift, weight_sum, values = combined(parts)
    lane = iota((8, HD), 1)
    extra = jnp.where(lane == 0, shift, jnp.where(lane == 1, weight_sum, 0.0))
    out_ref[...] = jnp.broadcast_to(jnp.concatenate([values, extra], axis=0)[None], out_ref.shape)
    n = parts.shape[0]
    source, place = iota((n, n * CAP), 0), iota((n, n * CAP), 1)
    ids = parts[:, 8, :]
    ids = jnp.where(place % CAP == 0, ids[:, 2:3], ids[:, 3:4])
    ids_ref[...] = jnp.sum(jnp.where(source == place // CAP, ids, 0.0), axis=0, keepdims=True).astype(jnp.int32)


def project_kernel(parts_ref, weight_ref, out_ref):
    _, weight_sum, values = combined(parts_ref[...])
    attended = (values / weight_sum).astype(BF16)
    total = jnp.zeros((8, weight_ref.shape[1]), F32)
    upper = jnp.dot(attended, weight_ref[:HD], preferred_element_type=F32)
    lower = jnp.dot(attended, weight_ref[HD:], preferred_element_type=F32)
    out_ref[...] = (upper[:B] + lower[B:]).astype(out_ref.dtype)


def pair_kernel(parts_ref, out_ref):
    both = jnp.sum(parts_ref[...].astype(F32), axis=0).astype(out_ref.dtype)
    out_ref[...] = jnp.broadcast_to(both[None], out_ref.shape)


def add_kernel(parts_ref, out_ref):
    out_ref[...] = jnp.sum(parts_ref[...].astype(F32), axis=0).astype(out_ref.dtype)


def local(queries, res_cache, res_count, move_cache, move_request, move_owner, out_weight):
    kv_size, tp_size = lax.axis_size("kv"), lax.axis_size("tp")
    owners = move_owner.reshape(-1)
    parts = pl.pallas_call(
        attend_kernel,
        out_shape=jax.ShapeDtypeStruct((kv_size, 16, HD), BF16),
        in_specs=[VMEM, VMEM, VMEM, SMEM, SMEM, VMEM, VMEM],
        out_specs=VMEM,
        name="attend",
    )(queries, res_cache, move_cache, res_count, move_request, owners[None, :], move_request[None, :])
    page = move_cache.shape[1:]

    def pages(n):
        return jax.ShapeDtypeStruct((n,) + page, BF16)

    def shift(x, chips):
        return lax.ppermute(x, "kv", [(i, (i + 2 * chips) % kv_size) for i in range(kv_size)])

    own, other = pl.pallas_call(
        pack_kernel,
        out_shape=(pages(CHIPS * CAP), pages(CHIPS * CAP)),
        in_specs=[VMEM, SMEM],
        out_specs=(VMEM, VMEM),
        scratch_shapes=[pltpu.SMEM((kv_size,), jnp.int32)],
        name="pack",
    )(move_cache, owners)
    got = lax.ppermute(other, "kv", [(i, i ^ 1) for i in range(kv_size)])
    parts = lax.all_to_all(parts, "kv", split_axis=0, concat_axis=0, tiled=True)
    up, down, far, near = pl.pallas_call(
        merge_kernel,
        out_shape=(pages(16), pages(16), pages(4), pages(28)),
        in_specs=[VMEM, VMEM],
        out_specs=(VMEM, VMEM, VMEM, VMEM),
        name="merge",
    )(own, got)
    up, down, far = shift(up, 4), shift(down, -4), shift(far, 8)
    part, landed_ids = pl.pallas_call(
        column_kernel,
        out_shape=(
            jax.ShapeDtypeStruct((tp_size, 16, HD), F32),
            jax.ShapeDtypeStruct((1, kv_size * CAP), jnp.int32),
        ),
        in_specs=[VMEM],
        out_specs=(VMEM, VMEM),
        name="column",
    )(parts)
    columns = lax.all_to_all(part, "tp", split_axis=0, concat_axis=0, tiled=True)
    partial_out = pl.pallas_call(
        project_kernel,
        out_shape=jax.ShapeDtypeStruct((B, out_weight.shape[1]), BF16),
        in_specs=[VMEM, VMEM],
        out_specs=VMEM,
        name="project",
    )(columns, out_weight)
    pair = lax.all_gather(partial_out, "kv", axis_index_groups=[[2 * z, 2 * z + 1] for z in range(CHIPS)])
    chip_out = pl.pallas_call(
        pair_kernel,
        out_shape=jax.ShapeDtypeStruct((CHIPS, B, out_weight.shape[1]), BF16),
        in_specs=[VMEM],
        out_specs=VMEM,
        name="pair",
    )(pair)
    partials = lax.all_to_all(
        chip_out,
        "kv",
        split_axis=0,
        concat_axis=0,
        tiled=True,
        axis_index_groups=[[2 * z + c for z in range(CHIPS)] for c in range(2)],
    )
    mixed = pl.pallas_call(
        add_kernel,
        out_shape=jax.ShapeDtypeStruct((B, out_weight.shape[1]), BF16),
        in_specs=[VMEM],
        out_specs=VMEM,
        name="add",
    )(partials)
    steps = pl.pallas_call(
        forward_kernel,
        out_shape=tuple(pages(8) for _ in range(6)),
        in_specs=[VMEM, VMEM, VMEM, pl.BlockSpec(memory_space=pl.ANY)],
        out_specs=(VMEM,) * 6,
        name="forward",
    )(near, up, down, partial_out)
    steps = [shift(x, (n // 2 + 1) * (1 - 2 * (n % 2))) for n, x in enumerate(steps)]
    landed = pl.pallas_call(
        land_kernel,
        out_shape=pages(kv_size * CAP),
        in_specs=[VMEM] * 10,
        out_specs=VMEM,
        name="land",
    )(near, up, down, far, *steps)
    return (mixed, landed, landed_ids.reshape(-1))


def solution(mesh):
    placed = (
        P(),
        P(("kv", "tp"), None, None, None),
        P(("kv", "tp"), None),
        P(("kv", "tp"), None, None, None),
        P(("kv", "tp")),
        P(("kv", "tp"), None),
        P("kv", "tp"),
    )
    return jax.shard_map(
        local,
        mesh=mesh,
        in_specs=placed,
        out_specs=(P(None, "tp"), P(("kv", "tp"), None, None, None), P(("kv", "tp"))),
        check_vma=False,
    )
```

```python
import math

import jax
import jax.numpy as jnp
from jax import lax
from jax.experimental import pallas as pl
from jax.experimental.pallas import tpu as pltpu
from jax.sharding import PartitionSpec as P

HQ = 64
KVH = 4
HD = 128
GROUP = 16
B = 4
PAGE = 8
CAP = 2
CHIPS = 16
NEG = -1e30

VMEM = pl.BlockSpec(memory_space=pltpu.VMEM)
ANY = pl.BlockSpec(memory_space=pl.ANY)
SMEM = pl.BlockSpec(memory_space=pltpu.SMEM)
F32 = jnp.float32
BF16 = jnp.bfloat16


def iota(shape, dim):
    return lax.broadcasted_iota(jnp.int32, shape, dim)


def round_up(x):
    return (x + jnp.abs(x) * 2.0**-7).astype(BF16).astype(F32)


def token_rows(ref, part):
    pages = ref[:, part].astype(F32)
    return pages.reshape(pages.shape[0] * PAGE, KVH * HD).astype(BF16)


def attend_kernel(q_ref, res_ref, move_ref, count_ref, request_ref, owner_ref, request_row_ref, out_ref):
    rows = GROUP * B
    n_res, n_move = res_ref.shape[0], move_ref.shape[0]
    page = iota((8, n_res * PAGE), 1) // PAGE
    end = jnp.int32(0)
    res_request = jnp.zeros_like(page)
    for b in range(B - 1):
        end = end + count_ref[0, b]
        res_request = res_request + (page >= end).astype(jnp.int32)
    page = iota((8, n_move * PAGE), 1) // PAGE
    move_request = jnp.zeros_like(page)
    for p in range(n_move):
        move_request = jnp.where(page == p, request_ref[p], move_request)
    token_request = jnp.concatenate([res_request, move_request], axis=1)
    wanted = iota((8, token_request.shape[1]), 0) % B == token_request
    wanted = jnp.concatenate([wanted.astype(F32)] * (rows // 8), axis=0) > 0.5

    keys = jnp.concatenate([token_rows(res_ref, 0), token_rows(move_ref, 0)], axis=0)
    values = jnp.concatenate([token_rows(res_ref, 1), token_rows(move_ref, 1)], axis=0)
    q = q_ref[...].astype(F32)

    owner = owner_ref[...]
    column = jnp.sum(
        jnp.where(iota((n_move, n_move), 0) == iota((n_move, n_move), 1), owner, 0), axis=1, keepdims=True
    )
    before = (column == owner) & (iota((n_move, n_move), 0) < iota((n_move, n_move), 1))
    rank = jnp.sum(before.astype(jnp.int32), axis=0, keepdims=True)
    all_rows = out_ref.shape[0] * 8
    named = iota((all_rows, n_move), 0) // 8 == owner
    marks = request_row_ref[...] + 1
    slot_ids = [
        (jnp.sum(jnp.where(named & (rank == r), marks, 0), axis=1, keepdims=True) - 1).astype(F32)
        for r in range(CAP)
    ]

    lane = iota((rows, HD), 1)
    per = rows // 8
    for g in range(KVH):
        heads = [q[:, (g * GROUP + i) * HD : (g * GROUP + i + 1) * HD] for i in range(GROUP)]
        q_rows = jnp.concatenate(heads, axis=0).astype(BF16)
        scores = lax.dot_general(
            q_rows, keys[:, g * HD : (g + 1) * HD], (((1,), (1,)), ((), ())), preferred_element_type=F32
        ) * (1.0 / math.sqrt(HD))
        scores = jnp.where(wanted, scores, NEG)
        shift = round_up(jnp.max(scores, axis=1, keepdims=True))
        weights = jnp.where(wanted, jnp.exp(scores - shift), 0.0).astype(BF16)
        weight_sum = jnp.sum(weights.astype(F32), axis=1, keepdims=True)
        summed = jnp.dot(weights, values[:, g * HD : (g + 1) * HD], preferred_element_type=F32)
        own = slice(g * rows, (g + 1) * rows)
        extra = jnp.where(lane == 0, shift, jnp.where(lane == 1, weight_sum, 0.0))
        for r in range(CAP):
            extra = jnp.where(lane == 2 + r, slot_ids[r][own], extra)
        both = jnp.concatenate([summed.reshape(per, 8, HD), extra.reshape(per, 8, HD)], axis=1)
        out_ref[g * per : (g + 1) * per] = both.astype(BF16)


CHUNK = 8
HALF = CHUNK // 2
FAR = 8
HOME = 4 * FAR
GIVEN = 4 * (FAR - 1)


def pack_kernel(move_ref, owner_ref, own_ref, other_ref, used_ref):
    own_ref[...] = jnp.zeros(own_ref.shape, own_ref.dtype)
    other_ref[...] = jnp.zeros(other_ref.shape, other_ref.dtype)
    for o in range(used_ref.shape[0]):
        used_ref[o] = 0
    me = lax.axis_index("kv")
    chip, core = me // 2, me % 2

    def place(p, carry):
        owner = owner_ref[p]
        rank = used_ref[owner]
        used_ref[owner] = rank + 1
        up = (owner // 2 - chip) & (CHIPS - 1)
        lands = owner % 2
        carrier = jnp.where(up == 0, lands, jnp.where(up == FAR, core, (up > FAR).astype(jnp.int32)))
        distance = jnp.where(up > FAR, CHIPS - up, up)
        slot = (distance - 1) * 4 + jnp.where(lands == carrier, 0, CAP) + rank
        home = jnp.where(carrier == core, HOME, GIVEN) + rank
        slot = jnp.where(up == 0, home, slot)

        @pl.when(carrier == core)
        def _():
            own_ref[slot] = move_ref[p]

        @pl.when(carrier != core)
        def _():
            other_ref[slot] = move_ref[p]

        return carry

    lax.fori_loop(0, move_ref.shape[0], place, 0)


def merge_kernel(own_ref, got_ref, three_ref, six_ref, near_ref):
    core = lax.axis_index("kv") % 2
    for ref, distances in ((three_ref, (3, 4, 5)), (six_ref, (6, 7)), (near_ref, (1, 2))):
        for n, distance in enumerate(distances):
            for end in range(2):
                source = slice((distance - 1) * 4 + end * CAP, (distance - 1) * 4 + (end + 1) * CAP)
                base = n * CHUNK + end * HALF
                ref[pl.ds(base + core * CAP, CAP)] = own_ref[source]
                ref[pl.ds(base + (1 - core) * CAP, CAP)] = got_ref[source]
    six_ref[2 * CHUNK :] = own_ref[(FAR - 1) * 4 : FAR * 4]


def forward_kernel(near_ref, three_ref, six_ref, after_ref, one_ref, two_ref):
    del after_ref
    for n, ref in enumerate((one_ref, two_ref)):
        last = CHUNK if n == 0 else HALF
        ref[:CHUNK] = near_ref[n * CHUNK : (n + 1) * CHUNK]
        ref[CHUNK : 2 * CHUNK] = three_ref[(n + 1) * CHUNK : (n + 2) * CHUNK]
        ref[2 * CHUNK :] = six_ref[(n + 1) * CHUNK : (n + 1) * CHUNK + last]


def arrived(three_ref, six_ref, one_ref, two_ref):
    return (
        (1, one_ref, 0),
        (2, two_ref, 0),
        (3, three_ref, 0),
        (4, one_ref, CHUNK),
        (5, two_ref, CHUNK),
        (6, six_ref, 0),
        (7, one_ref, 2 * CHUNK),
    )


def give_kernel(three_ref, six_ref, one_ref, two_ref, out_ref):
    for distance, ref, first in arrived(three_ref, six_ref, one_ref, two_ref):
        out_ref[(distance - 1) * HALF : distance * HALF] = ref[first + HALF : first + CHUNK]
    out_ref[GIVEN:] = two_ref[2 * CHUNK + CAP :]


def land_kernel(own_ref, got_ref, three_ref, six_ref, one_ref, two_ref, taken_ref, out_ref):
    me = lax.axis_index("kv")
    chip, core = me // 2, me % 2
    way = 1 - 2 * core

    def first_row(up):
        return ((chip + up) & (CHIPS - 1)) * HALF

    out_ref[pl.ds(first_row(0) + core * CAP, CAP)] = own_ref[HOME:]
    out_ref[pl.ds(first_row(0) + (1 - core) * CAP, CAP)] = got_ref[GIVEN:]
    out_ref[pl.ds(first_row(FAR) + core * CAP, CAP)] = two_ref[2 * CHUNK : 2 * CHUNK + CAP]
    out_ref[pl.ds(first_row(FAR) + (1 - core) * CAP, CAP)] = taken_ref[GIVEN:]
    for distance, ref, first in arrived(three_ref, six_ref, one_ref, two_ref):
        out_ref[pl.ds(first_row(-way * distance), HALF)] = ref[first : first + HALF]
        out_ref[pl.ds(first_row(way * distance), HALF)] = taken_ref[(distance - 1) * HALF : distance * HALF]


def combined(parts):
    shifts, sums, values = parts[:, 8:, 0:1], parts[:, 8:, 1:2], parts[:, :8, :]
    shift = jnp.max(shifts, axis=0)
    factor = jnp.exp(shifts - shift[None])
    return shift, jnp.sum(sums * factor, axis=0), jnp.sum(values * factor, axis=0)


def column_kernel(parts_ref, after_ref, out_ref, ids_ref):
    del after_ref
    parts = parts_ref[...].astype(F32)
    shift, weight_sum, values = combined(parts)
    lane = iota((8, HD), 1)
    extra = jnp.where(lane == 0, shift, jnp.where(lane == 1, weight_sum, 0.0))
    out_ref[...] = jnp.broadcast_to(jnp.concatenate([values, extra], axis=0)[None], out_ref.shape)
    n = parts.shape[0]
    source, place = iota((n, n * CAP), 0), iota((n, n * CAP), 1)
    ids = parts[:, 8, :]
    ids = jnp.where(place % CAP == 0, ids[:, 2:3], ids[:, 3:4])
    ids_ref[...] = jnp.sum(jnp.where(source == place // CAP, ids, 0.0), axis=0, keepdims=True).astype(jnp.int32)


def project_kernel(parts_ref, weight_ref, out_ref):
    _, weight_sum, values = combined(parts_ref[...])
    attended = (values / weight_sum).astype(BF16)
    total = jnp.zeros((8, weight_ref.shape[1]), F32)
    upper = jnp.dot(attended, weight_ref[:HD], preferred_element_type=F32)
    lower = jnp.dot(attended, weight_ref[HD:], preferred_element_type=F32)
    out_ref[...] = (upper[:B] + lower[B:]).astype(out_ref.dtype)


def pair_kernel(parts_ref, out_ref):
    both = jnp.sum(parts_ref[...].astype(F32), axis=0).astype(out_ref.dtype)
    out_ref[...] = jnp.broadcast_to(both[None], out_ref.shape)


def add_kernel(parts_ref, out_ref):
    out_ref[...] = jnp.sum(parts_ref[...].astype(F32), axis=0).astype(out_ref.dtype)


def local(queries, res_cache, res_count, move_cache, move_request, move_owner, out_weight):
    kv_size, tp_size = lax.axis_size("kv"), lax.axis_size("tp")
    owners = move_owner.reshape(-1)
    parts = pl.pallas_call(
        attend_kernel,
        out_shape=jax.ShapeDtypeStruct((kv_size, 16, HD), BF16),
        in_specs=[VMEM, VMEM, VMEM, SMEM, SMEM, VMEM, VMEM],
        out_specs=VMEM,
        name="attend",
    )(queries, res_cache, move_cache, res_count, move_request, owners[None, :], move_request[None, :])
    page = move_cache.shape[1:]

    def pages(n):
        return jax.ShapeDtypeStruct((n,) + page, BF16)

    def shift(x, chips):
        pairs = [(i, (i + 2 * chips * (1 - 2 * (i % 2))) % kv_size) for i in range(kv_size)]
        return lax.ppermute(x, "kv", pairs)

    def swap(x):
        return lax.ppermute(x, "kv", [(i, i ^ 1) for i in range(kv_size)])

    own, other = pl.pallas_call(
        pack_kernel,
        out_shape=(pages(HOME + CAP), pages(GIVEN + CAP)),
        in_specs=[VMEM, SMEM],
        out_specs=(VMEM, VMEM),
        scratch_shapes=[pltpu.SMEM((kv_size,), jnp.int32)],
        name="pack",
    )(move_cache, owners)
    got = swap(other)
    parts = lax.all_to_all(parts, "kv", split_axis=0, concat_axis=0, tiled=True)
    three, six, near = pl.pallas_call(
        merge_kernel,
        out_shape=(pages(3 * CHUNK), pages(2 * CHUNK + HALF), pages(2 * CHUNK)),
        in_specs=[VMEM, VMEM],
        out_specs=(VMEM, VMEM, VMEM),
        name="merge",
    )(own, got)
    six, three = shift(six, 6), shift(three, 3)
    part, landed_ids = pl.pallas_call(
        column_kernel,
        out_shape=(
            jax.ShapeDtypeStruct((tp_size, 16, HD), F32),
            jax.ShapeDtypeStruct((1, kv_size * CAP), jnp.int32),
        ),
        in_specs=[VMEM, ANY],
        out_specs=(VMEM, VMEM),
        name="column",
    )(parts, near)
    columns = lax.all_to_all(part, "tp", split_axis=0, concat_axis=0, tiled=True)
    partial_out = pl.pallas_call(
        project_kernel,
        out_shape=jax.ShapeDtypeStruct((B, out_weight.shape[1]), BF16),
        in_specs=[VMEM, VMEM],
        out_specs=VMEM,
        name="project",
    )(columns, out_weight)
    pair = lax.all_gather(partial_out, "kv", axis_index_groups=[[2 * z, 2 * z + 1] for z in range(CHIPS)])
    chip_out = pl.pallas_call(
        pair_kernel,
        out_shape=jax.ShapeDtypeStruct((CHIPS, B, out_weight.shape[1]), BF16),
        in_specs=[VMEM],
        out_specs=VMEM,
        name="pair",
    )(pair)
    partials = lax.all_to_all(
        chip_out,
        "kv",
        split_axis=0,
        concat_axis=0,
        tiled=True,
        axis_index_groups=[[2 * z + c for z in range(CHIPS)] for c in range(2)],
    )
    mixed = pl.pallas_call(
        add_kernel,
        out_shape=jax.ShapeDtypeStruct((B, out_weight.shape[1]), BF16),
        in_specs=[VMEM],
        out_specs=VMEM,
        name="add",
    )(partials)
    one, two = pl.pallas_call(
        forward_kernel,
        out_shape=(pages(3 * CHUNK), pages(2 * CHUNK + HALF)),
        in_specs=[VMEM, VMEM, VMEM, ANY],
        out_specs=(VMEM, VMEM),
        name="forward",
    )(near, three, six, chip_out)
    two, one = shift(two, 2), shift(one, 1)
    give = pl.pallas_call(
        give_kernel,
        out_shape=pages(GIVEN + CAP),
        in_specs=[VMEM] * 4,
        out_specs=VMEM,
        name="give",
    )(three, six, one, two)
    taken = swap(give)
    landed = pl.pallas_call(
        land_kernel,
        out_shape=pages(kv_size * CAP),
        in_specs=[VMEM] * 7,
        out_specs=VMEM,
        name="land",
    )(own, got, three, six, one, two, taken)
    return (mixed, landed, landed_ids.reshape(-1))


def solution(mesh):
    placed = (
        P(),
        P(("kv", "tp"), None, None, None),
        P(("kv", "tp"), None),
        P(("kv", "tp"), None, None, None),
        P(("kv", "tp")),
        P(("kv", "tp"), None),
        P("kv", "tp"),
    )
    return jax.shard_map(
        local,
        mesh=mesh,
        in_specs=placed,
        out_specs=(P(None, "tp"), P(("kv", "tp"), None, None, None), P(("kv", "tp"))),
        check_vma=False,
    )
```

```python
import math

import jax
import jax.numpy as jnp
from jax import lax
from jax.experimental import pallas as pl
from jax.experimental.pallas import tpu as pltpu
from jax.sharding import PartitionSpec as P

HQ = 64
KVH = 4
HD = 128
GROUP = 16
B = 4
PAGE = 8
CAP = 2
CHIPS = 16
NEG = -1e30
SMALL = 8 * 2**20

VMEM = pl.BlockSpec(memory_space=pltpu.VMEM)
ANY = pl.BlockSpec(memory_space=pl.ANY)
SMEM = pl.BlockSpec(memory_space=pltpu.SMEM)
F32 = jnp.float32
BF16 = jnp.bfloat16


def iota(shape, dim):
    return lax.broadcasted_iota(jnp.int32, shape, dim)


def round_up(x):
    return (x + jnp.abs(x) * 2.0**-7).astype(BF16).astype(F32)


def token_rows(ref, part):
    pages = ref[:, part].astype(F32)
    return pages.reshape(pages.shape[0] * PAGE, KVH * HD).astype(BF16)


def attend_kernel(q_ref, res_ref, move_ref, count_ref, request_ref, owner_ref, request_row_ref, out_ref):
    rows = GROUP * B
    n_res, n_move = res_ref.shape[0], move_ref.shape[0]
    page = iota((8, n_res * PAGE), 1) // PAGE
    end = jnp.int32(0)
    res_request = jnp.zeros_like(page)
    for b in range(B - 1):
        end = end + count_ref[0, b]
        res_request = res_request + (page >= end).astype(jnp.int32)
    page = iota((8, n_move * PAGE), 1) // PAGE
    move_request = jnp.zeros_like(page)
    for p in range(n_move):
        move_request = jnp.where(page == p, request_ref[p], move_request)
    token_request = jnp.concatenate([res_request, move_request], axis=1)
    wanted = iota((8, token_request.shape[1]), 0) % B == token_request
    wanted = jnp.concatenate([wanted.astype(F32)] * (rows // 8), axis=0) > 0.5

    keys = jnp.concatenate([token_rows(res_ref, 0), token_rows(move_ref, 0)], axis=0)
    values = jnp.concatenate([token_rows(res_ref, 1), token_rows(move_ref, 1)], axis=0)
    q = q_ref[...].astype(F32)

    owner = owner_ref[...]
    column = jnp.sum(
        jnp.where(iota((n_move, n_move), 0) == iota((n_move, n_move), 1), owner, 0), axis=1, keepdims=True
    )
    before = (column == owner) & (iota((n_move, n_move), 0) < iota((n_move, n_move), 1))
    rank = jnp.sum(before.astype(jnp.int32), axis=0, keepdims=True)
    all_rows = out_ref.shape[0] * 8
    named = iota((all_rows, n_move), 0) // 8 == owner
    marks = request_row_ref[...] + 1
    slot_ids = [
        (jnp.sum(jnp.where(named & (rank == r), marks, 0), axis=1, keepdims=True) - 1).astype(F32)
        for r in range(CAP)
    ]

    lane = iota((rows, HD), 1)
    per = rows // 8
    for g in range(KVH):
        heads = [q[:, (g * GROUP + i) * HD : (g * GROUP + i + 1) * HD] for i in range(GROUP)]
        q_rows = jnp.concatenate(heads, axis=0).astype(BF16)
        scores = lax.dot_general(
            q_rows, keys[:, g * HD : (g + 1) * HD], (((1,), (1,)), ((), ())), preferred_element_type=F32
        ) * (1.0 / math.sqrt(HD))
        scores = jnp.where(wanted, scores, NEG)
        shift = round_up(jnp.max(scores, axis=1, keepdims=True))
        weights = jnp.where(wanted, jnp.exp(scores - shift), 0.0).astype(BF16)
        weight_sum = jnp.sum(weights.astype(F32), axis=1, keepdims=True)
        summed = jnp.dot(weights, values[:, g * HD : (g + 1) * HD], preferred_element_type=F32)
        own = slice(g * rows, (g + 1) * rows)
        extra = jnp.where(lane == 0, shift, jnp.where(lane == 1, weight_sum, 0.0))
        for r in range(CAP):
            extra = jnp.where(lane == 2 + r, slot_ids[r][own], extra)
        both = jnp.concatenate([summed.reshape(per, 8, HD), extra.reshape(per, 8, HD)], axis=1)
        out_ref[g * per : (g + 1) * per] = both.astype(BF16)


FAR = 8
QUAD = 4
HOME = QUAD * FAR
GIVEN = QUAD * (FAR - 1)


def copy_all(copies, sems):
    running = [pltpu.make_async_copy(a, b, sems.at[n]) for n, (a, b) in enumerate(copies)]
    for copy in running:
        copy.start()
    for copy in running:
        copy.wait()


def quads(ref, first, count=1):
    return ref.at[pl.ds(first * QUAD, count * QUAD)]


def pack_kernel(move_ref, owner_ref, own_ref, other_ref, used_ref):
    own_ref[...] = jnp.zeros(own_ref.shape, own_ref.dtype)
    other_ref[...] = jnp.zeros(other_ref.shape, other_ref.dtype)
    for o in range(used_ref.shape[0]):
        used_ref[o] = 0
    me = lax.axis_index("kv")
    chip, core = me // 2, me % 2

    def place(p, carry):
        owner = owner_ref[p]
        rank = used_ref[owner]
        used_ref[owner] = rank + 1
        up = (owner // 2 - chip) & (CHIPS - 1)
        lands = owner % 2
        carrier = jnp.where(up == 0, lands, jnp.where(up == FAR, core, (up > FAR).astype(jnp.int32)))
        distance = jnp.where(up > FAR, CHIPS - up, up)
        slot = (distance - 1) * 4 + jnp.where(lands == carrier, 0, CAP) + rank
        home = jnp.where(carrier == core, HOME, GIVEN) + rank
        slot = jnp.where(up == 0, home, slot)

        @pl.when(carrier == core)
        def _():
            own_ref[slot] = move_ref[p]

        @pl.when(carrier != core)
        def _():
            other_ref[slot] = move_ref[p]

        return carry

    lax.fori_loop(0, move_ref.shape[0], place, 0)


def merge_kernel(own_ref, got_ref, three_ref, six_ref, sems):
    copy_all(
        [
            (quads(own_ref, 5, 3), quads(six_ref, 0, 3)),
            (quads(got_ref, 5, 2), quads(six_ref, 3, 2)),
            (quads(own_ref, 2, 3), quads(three_ref, 0, 3)),
            (quads(got_ref, 2, 3), quads(three_ref, 3, 3)),
        ],
        sems,
    )


def forward_kernel(own_ref, got_ref, three_ref, six_ref, after_ref, one_ref, two_ref, sems):
    del after_ref
    copies = []
    for n, ref in enumerate((one_ref, two_ref)):
        parts = [(own_ref, n), (got_ref, n), (three_ref, 1 + n), (three_ref, 4 + n), (six_ref, 1 + n)]
        parts += [(six_ref, 4)] if n == 0 else []
        copies += [(quads(source, first), quads(ref, to)) for to, (source, first) in enumerate(parts)]
    copy_all(copies, sems)


def arrived(three_ref, six_ref, one_ref, two_ref):
    return (
        (1, one_ref, 0, 1),
        (2, two_ref, 0, 1),
        (3, three_ref, 0, 3),
        (4, one_ref, 2, 3),
        (5, two_ref, 2, 3),
        (6, six_ref, 0, 3),
        (7, one_ref, 4, 5),
    )


def give_kernel(three_ref, six_ref, one_ref, two_ref, out_ref, sems):
    core = lax.axis_index("kv") % 2
    copies = [(two_ref.at[pl.ds(4 * QUAD + CAP, CAP)], out_ref.at[pl.ds(GIVEN, CAP)])]
    for distance, ref, same, other in arrived(three_ref, six_ref, one_ref, two_ref):
        for quad, start in ((same, core), (other, 1 - core)):
            to = out_ref.at[pl.ds((distance - 1) * QUAD + start * CAP, CAP)]
            copies.append((ref.at[pl.ds(quad * QUAD + CAP, CAP)], to))
    copy_all(copies, sems)


def land_kernel(own_ref, got_ref, three_ref, six_ref, one_ref, two_ref, taken_ref, out_ref, sems):
    me = lax.axis_index("kv")
    chip, core = me // 2, me % 2
    way = 1 - 2 * core

    def rows(up, start):
        return out_ref.at[pl.ds(((chip + up) & (CHIPS - 1)) * QUAD + start * CAP, CAP)]

    copies = [
        (own_ref.at[pl.ds(HOME, CAP)], rows(0, core)),
        (got_ref.at[pl.ds(GIVEN, CAP)], rows(0, 1 - core)),
        (two_ref.at[pl.ds(4 * QUAD, CAP)], rows(FAR, core)),
        (taken_ref.at[pl.ds(GIVEN, CAP)], rows(FAR, 1 - core)),
    ]
    for distance, ref, same, other in arrived(three_ref, six_ref, one_ref, two_ref):
        for quad, start in ((same, core), (other, 1 - core)):
            copies.append((ref.at[pl.ds(quad * QUAD, CAP)], rows(-way * distance, start)))
        to = out_ref.at[pl.ds(((chip + way * distance) & (CHIPS - 1)) * QUAD, QUAD)]
        copies.append((quads(taken_ref, distance - 1), to))
    copy_all(copies, sems)


def combined(parts):
    shifts, sums, values = parts[:, 8:, 0:1], parts[:, 8:, 1:2], parts[:, :8, :]
    shift = jnp.max(shifts, axis=0)
    factor = jnp.exp(shifts - shift[None])
    return shift, jnp.sum(sums * factor, axis=0), jnp.sum(values * factor, axis=0)


def column_kernel(parts_any, after_ref, out_ref, ids_ref, parts_ref):
    del after_ref
    pltpu.sync_copy(parts_any, parts_ref)
    parts = parts_ref[...].astype(F32)
    shift, weight_sum, values = combined(parts)
    lane = iota((8, HD), 1)
    extra = jnp.where(lane == 0, shift, jnp.where(lane == 1, weight_sum, 0.0))
    out_ref[...] = jnp.broadcast_to(jnp.concatenate([values, extra], axis=0)[None], out_ref.shape)
    n = parts.shape[0]
    source, place = iota((n, n * CAP), 0), iota((n, n * CAP), 1)
    ids = parts[:, 8, :]
    ids = jnp.where(place % CAP == 0, ids[:, 2:3], ids[:, 3:4])
    ids_ref[...] = jnp.sum(jnp.where(source == place // CAP, ids, 0.0), axis=0, keepdims=True).astype(jnp.int32)


def project_kernel(parts_any, weight_ref, out_ref, parts_ref):
    pltpu.sync_copy(parts_any, parts_ref)
    _, weight_sum, values = combined(parts_ref[...])
    attended = (values / weight_sum).astype(BF16)
    upper = jnp.dot(attended, weight_ref[:HD], preferred_element_type=F32)
    lower = jnp.dot(attended, weight_ref[HD:], preferred_element_type=F32)
    partial = (upper[:B] + lower[B:]).astype(out_ref.dtype)
    out_ref[...] = jnp.broadcast_to(partial[None], out_ref.shape)


def add_kernel(parts_any, out_ref, parts_ref):
    pltpu.sync_copy(parts_any, parts_ref)
    out_ref[...] = jnp.sum(parts_ref[...].astype(F32), axis=0).astype(out_ref.dtype)


def local(queries, res_cache, res_count, move_cache, move_request, move_owner, out_weight):
    kv_size, tp_size = lax.axis_size("kv"), lax.axis_size("tp")
    owners = move_owner.reshape(-1)
    parts = pl.pallas_call(
        attend_kernel,
        out_shape=jax.ShapeDtypeStruct((kv_size, 16, HD), BF16),
        in_specs=[VMEM, VMEM, VMEM, SMEM, SMEM, VMEM, VMEM],
        out_specs=VMEM,
        name="attend",
    )(queries, res_cache, move_cache, res_count, move_request, owners[None, :], move_request[None, :])
    page = move_cache.shape[1:]

    def pages(n):
        return jax.ShapeDtypeStruct((n,) + page, BF16)

    def shift(x, chips):
        pairs = [(i, (i + 2 * chips * (1 - 2 * (i % 2))) % kv_size) for i in range(kv_size)]
        return lax.ppermute(x, "kv", pairs)

    def swap(x):
        return lax.ppermute(x, "kv", [(i, i ^ 1) for i in range(kv_size)])

    own, other = pl.pallas_call(
        pack_kernel,
        out_shape=(pages(HOME + CAP), pages(GIVEN + CAP)),
        in_specs=[VMEM, SMEM],
        out_specs=(VMEM, VMEM),
        scratch_shapes=[pltpu.SMEM((kv_size,), jnp.int32)],
        name="pack",
    )(move_cache, owners)
    got = swap(other)
    parts = lax.all_to_all(parts, "kv", split_axis=0, concat_axis=0, tiled=True)
    def copies(kernel, name, out_pages, count, *args):
        return pl.pallas_call(
            kernel,
            out_shape=tuple(pages(n) for n in out_pages),
            in_specs=[ANY] * len(args),
            out_specs=(ANY,) * len(out_pages),
            scratch_shapes=[pltpu.SemaphoreType.DMA((count,))],
            compiler_params=pltpu.CompilerParams(vmem_limit_bytes=SMALL),
            cost_estimate=pl.CostEstimate(flops=0, bytes_accessed=1024, transcendentals=0),
            name=name,
        )(*args)

    three, six = copies(merge_kernel, "merge", (6 * QUAD, 5 * QUAD), 4, own, got)
    six_up, three_up = shift(six, 6), shift(three, 3)
    part, landed_ids = pl.pallas_call(
        column_kernel,
        out_shape=(
            jax.ShapeDtypeStruct((tp_size, 16, HD), F32),
            jax.ShapeDtypeStruct((1, kv_size * CAP), jnp.int32),
        ),
        in_specs=[ANY, ANY],
        out_specs=(VMEM, VMEM),
        scratch_shapes=[pltpu.VMEM(parts.shape, BF16)],
        compiler_params=pltpu.CompilerParams(vmem_limit_bytes=SMALL),
        name="column",
    )(parts, three)
    three, six = three_up, six_up
    columns = lax.all_to_all(part, "tp", split_axis=0, concat_axis=0, tiled=True)
    partial_out = pl.pallas_call(
        project_kernel,
        out_shape=jax.ShapeDtypeStruct((kv_size, B, out_weight.shape[1]), BF16),
        in_specs=[ANY, VMEM],
        out_specs=VMEM,
        scratch_shapes=[pltpu.VMEM(columns.shape, F32)],
        compiler_params=pltpu.CompilerParams(vmem_limit_bytes=SMALL),
        name="project",
    )(columns, out_weight)
    partials = lax.all_to_all(partial_out, "kv", split_axis=0, concat_axis=0, tiled=True)
    mixed = pl.pallas_call(
        add_kernel,
        out_shape=jax.ShapeDtypeStruct((B, out_weight.shape[1]), BF16),
        in_specs=[ANY],
        out_specs=VMEM,
        scratch_shapes=[pltpu.VMEM(partials.shape, BF16)],
        compiler_params=pltpu.CompilerParams(vmem_limit_bytes=SMALL),
        name="add",
    )(partials)
    one, two = copies(forward_kernel, "forward", (6 * QUAD, 5 * QUAD), 11, own, got, three, six, partial_out)
    two, one = shift(two, 2), shift(one, 1)
    (give,) = copies(give_kernel, "give", (GIVEN + CAP,), 15, three, six, one, two)
    taken = swap(give)
    (landed,) = copies(land_kernel, "land", (kv_size * CAP,), 25, own, got, three, six, one, two, taken)
    return (mixed, landed, landed_ids.reshape(-1))


def solution(mesh):
    placed = (
        P(),
        P(("kv", "tp"), None, None, None),
        P(("kv", "tp"), None),
        P(("kv", "tp"), None, None, None),
        P(("kv", "tp")),
        P(("kv", "tp"), None),
        P("kv", "tp"),
    )
    return jax.shard_map(
        local,
        mesh=mesh,
        in_specs=placed,
        out_specs=(P(None, "tp"), P(("kv", "tp"), None, None, None), P(("kv", "tp"))),
        check_vma=False,
    )
```

```python
import math

import jax
import jax.numpy as jnp
from jax import lax
from jax.experimental import pallas as pl
from jax.experimental.pallas import tpu as pltpu
from jax.sharding import PartitionSpec as P

HQ = 64
KVH = 4
HD = 128
GROUP = 16
B = 4
PAGE = 8
CAP = 2
CHIPS = 16
NEG = -1e30
SMALL = 8 * 2**20

VMEM = pl.BlockSpec(memory_space=pltpu.VMEM)
ANY = pl.BlockSpec(memory_space=pl.ANY)
SMEM = pl.BlockSpec(memory_space=pltpu.SMEM)
F32 = jnp.float32
BF16 = jnp.bfloat16


def iota(shape, dim):
    return lax.broadcasted_iota(jnp.int32, shape, dim)


def round_up(x):
    return (x + jnp.abs(x) * 2.0**-7).astype(BF16).astype(F32)


def token_rows(ref, part):
    pages = ref[:, part].astype(F32)
    return pages.reshape(pages.shape[0] * PAGE, KVH * HD).astype(BF16)


def side_lanes(lane, shift, weight_sum):
    high = weight_sum.astype(BF16).astype(F32)
    return jnp.where(lane == 0, shift, jnp.where(lane == 1, high, jnp.where(lane == 4, weight_sum - high, 0.0)))


def attend_kernel(q_ref, res_ref, move_ref, count_ref, request_ref, owner_ref, request_row_ref, out_ref):
    rows = GROUP * B
    n_res, n_move = res_ref.shape[0], move_ref.shape[0]
    page = iota((8, n_res * PAGE), 1) // PAGE
    end = jnp.int32(0)
    res_request = jnp.zeros_like(page)
    for b in range(B - 1):
        end = end + count_ref[0, b]
        res_request = res_request + (page >= end).astype(jnp.int32)
    page = iota((8, n_move * PAGE), 1) // PAGE
    move_request = jnp.zeros_like(page)
    for p in range(n_move):
        move_request = jnp.where(page == p, request_ref[p], move_request)
    token_request = jnp.concatenate([res_request, move_request], axis=1)
    wanted = iota((8, token_request.shape[1]), 0) % B == token_request
    wanted = jnp.concatenate([wanted.astype(F32)] * (rows // 8), axis=0) > 0.5

    keys = jnp.concatenate([token_rows(res_ref, 0), token_rows(move_ref, 0)], axis=0)
    values = jnp.concatenate([token_rows(res_ref, 1), token_rows(move_ref, 1)], axis=0)
    q = q_ref[...].astype(F32)

    owner = owner_ref[...]
    column = jnp.sum(
        jnp.where(iota((n_move, n_move), 0) == iota((n_move, n_move), 1), owner, 0), axis=1, keepdims=True
    )
    before = (column == owner) & (iota((n_move, n_move), 0) < iota((n_move, n_move), 1))
    rank = jnp.sum(before.astype(jnp.int32), axis=0, keepdims=True)
    all_rows = out_ref.shape[0] * 8
    named = iota((all_rows, n_move), 0) // 8 == owner
    marks = request_row_ref[...] + 1
    slot_ids = [
        (jnp.sum(jnp.where(named & (rank == r), marks, 0), axis=1, keepdims=True) - 1).astype(F32)
        for r in range(CAP)
    ]

    lane = iota((rows, HD), 1)
    per = rows // 8
    for g in range(KVH):
        heads = [q[:, (g * GROUP + i) * HD : (g * GROUP + i + 1) * HD] for i in range(GROUP)]
        q_rows = jnp.concatenate(heads, axis=0).astype(BF16)
        scores = lax.dot_general(
            q_rows, keys[:, g * HD : (g + 1) * HD], (((1,), (1,)), ((), ())), preferred_element_type=F32
        ) * (1.0 / math.sqrt(HD))
        scores = jnp.where(wanted, scores, NEG)
        shift = round_up(jnp.max(scores, axis=1, keepdims=True))
        weights = jnp.where(wanted, jnp.exp(scores - shift), 0.0).astype(BF16)
        weight_sum = jnp.sum(weights.astype(F32), axis=1, keepdims=True)
        summed = jnp.dot(weights, values[:, g * HD : (g + 1) * HD], preferred_element_type=F32)
        own = slice(g * rows, (g + 1) * rows)
        extra = side_lanes(lane, shift, weight_sum)
        for r in range(CAP):
            extra = jnp.where(lane == 2 + r, slot_ids[r][own], extra)
        both = jnp.concatenate([summed.reshape(per, 8, HD), extra.reshape(per, 8, HD)], axis=1)
        out_ref[g * per : (g + 1) * per] = both.astype(BF16)


FAR = 8
QUAD = 4
HOME = QUAD * FAR
GIVEN = QUAD * (FAR - 1)


def copy_all(copies, sems):
    running = [pltpu.make_async_copy(a, b, sems.at[n]) for n, (a, b) in enumerate(copies)]
    for copy in running:
        copy.start()
    for copy in running:
        copy.wait()


def quads(ref, first, count=1):
    return ref.at[pl.ds(first * QUAD, count * QUAD)]


def pack_kernel(move_ref, owner_ref, after_ref, own_ref, other_ref, used_ref):
    del after_ref
    own_ref[...] = jnp.zeros(own_ref.shape, own_ref.dtype)
    other_ref[...] = jnp.zeros(other_ref.shape, other_ref.dtype)
    for o in range(used_ref.shape[0]):
        used_ref[o] = 0
    me = lax.axis_index("kv")
    chip, core = me // 2, me % 2

    def place(p, carry):
        owner = owner_ref[p]
        rank = used_ref[owner]
        used_ref[owner] = rank + 1
        up = (owner // 2 - chip) & (CHIPS - 1)
        lands = owner % 2
        carrier = jnp.where(up == 0, lands, jnp.where(up == FAR, core, (up > FAR).astype(jnp.int32)))
        distance = jnp.where(up > FAR, CHIPS - up, up)
        slot = (distance - 1) * 4 + jnp.where(lands == carrier, 0, CAP) + rank
        home = jnp.where(carrier == core, HOME, GIVEN) + rank
        slot = jnp.where(up == 0, home, slot)

        @pl.when(carrier == core)
        def _():
            own_ref[slot] = move_ref[p]

        @pl.when(carrier != core)
        def _():
            other_ref[slot] = move_ref[p]

        return carry

    lax.fori_loop(0, move_ref.shape[0], place, 0)


def merge_six_kernel(own_ref, got_ref, out_ref, sems):
    pairs = [(quads(own_ref, 5, 3), quads(out_ref, 0, 3)), (quads(got_ref, 5, 2), quads(out_ref, 3, 2))]
    copy_all(pairs, sems)


def merge_three_kernel(own_ref, got_ref, after_ref, out_ref, sems):
    del after_ref
    pairs = [(quads(own_ref, 2, 3), quads(out_ref, 0, 3)), (quads(got_ref, 2, 3), quads(out_ref, 3, 3))]
    copy_all(pairs, sems)


def forward_kernel(own_ref, got_ref, three_ref, six_ref, after_ref, one_ref, two_ref, sems):
    del after_ref
    copies = []
    for n, ref in enumerate((one_ref, two_ref)):
        parts = [(own_ref, n), (got_ref, n), (three_ref, 1 + n), (three_ref, 4 + n), (six_ref, 1 + n)]
        parts += [(six_ref, 4)] if n == 0 else []
        copies += [(quads(source, first), quads(ref, to)) for to, (source, first) in enumerate(parts)]
    copy_all(copies, sems)


def arrived(three_ref, six_ref, one_ref, two_ref):
    return (
        (1, one_ref, 0, 1),
        (2, two_ref, 0, 1),
        (3, three_ref, 0, 3),
        (4, one_ref, 2, 3),
        (5, two_ref, 2, 3),
        (6, six_ref, 0, 3),
        (7, one_ref, 4, 5),
    )


def give_kernel(three_ref, six_ref, one_ref, two_ref, after_ref, out_ref, sems):
    del after_ref
    core = lax.axis_index("kv") % 2
    copies = [(two_ref.at[pl.ds(4 * QUAD + CAP, CAP)], out_ref.at[pl.ds(GIVEN, CAP)])]
    for distance, ref, same, other in arrived(three_ref, six_ref, one_ref, two_ref):
        for quad, start in ((same, core), (other, 1 - core)):
            to = out_ref.at[pl.ds((distance - 1) * QUAD + start * CAP, CAP)]
            copies.append((ref.at[pl.ds(quad * QUAD + CAP, CAP)], to))
    copy_all(copies, sems)


def land_kernel(own_ref, got_ref, three_ref, six_ref, one_ref, two_ref, taken_ref, out_ref, sems):
    me = lax.axis_index("kv")
    chip, core = me // 2, me % 2
    way = 1 - 2 * core

    def rows(up, start):
        return out_ref.at[pl.ds(((chip + up) & (CHIPS - 1)) * QUAD + start * CAP, CAP)]

    copies = [
        (own_ref.at[pl.ds(HOME, CAP)], rows(0, core)),
        (got_ref.at[pl.ds(GIVEN, CAP)], rows(0, 1 - core)),
        (two_ref.at[pl.ds(4 * QUAD, CAP)], rows(FAR, core)),
        (taken_ref.at[pl.ds(GIVEN, CAP)], rows(FAR, 1 - core)),
    ]
    for distance, ref, same, other in arrived(three_ref, six_ref, one_ref, two_ref):
        for quad, start in ((same, core), (other, 1 - core)):
            copies.append((ref.at[pl.ds(quad * QUAD, CAP)], rows(-way * distance, start)))
        to = out_ref.at[pl.ds(((chip + way * distance) & (CHIPS - 1)) * QUAD, QUAD)]
        copies.append((quads(taken_ref, distance - 1), to))
    copy_all(copies, sems)


def combined(parts):
    shifts, values = parts[:, 8:, 0:1], parts[:, :8, :]
    sums = parts[:, 8:, 1:2] + parts[:, 8:, 4:5]
    shift = jnp.max(shifts, axis=0)
    factor = jnp.exp(shifts - shift[None])
    return shift, jnp.sum(sums * factor, axis=0), jnp.sum(values * factor, axis=0)


def column_kernel(parts_any, after_ref, out_ref, ids_ref, parts_ref):
    del after_ref
    pltpu.sync_copy(parts_any, parts_ref)
    parts = parts_ref[...].astype(F32)
    shift, weight_sum, values = combined(parts)
    lane = iota((8, HD), 1)
    extra = side_lanes(lane, shift, weight_sum)
    out = jnp.concatenate([values, extra], axis=0).astype(out_ref.dtype)
    out_ref[...] = jnp.broadcast_to(out[None], out_ref.shape)
    n = parts.shape[0]
    source, place = iota((n, n * CAP), 0), iota((n, n * CAP), 1)
    ids = parts[:, 8, :]
    ids = jnp.where(place % CAP == 0, ids[:, 2:3], ids[:, 3:4])
    ids_ref[...] = jnp.sum(jnp.where(source == place // CAP, ids, 0.0), axis=0, keepdims=True).astype(jnp.int32)


def project_kernel(parts_any, weight_ref, out_ref, parts_ref):
    pltpu.sync_copy(parts_any, parts_ref)
    _, weight_sum, values = combined(parts_ref[...].astype(F32))
    attended = (values / weight_sum).astype(BF16)
    upper = jnp.dot(attended, weight_ref[:HD], preferred_element_type=F32)
    lower = jnp.dot(attended, weight_ref[HD:], preferred_element_type=F32)
    partial = (upper[:B] + lower[B:]).astype(out_ref.dtype)
    half = partial.shape[1] // 2
    for core in range(2):
        part = partial[:, core * half : (core + 1) * half]
        out_ref[:, core] = jnp.broadcast_to(part[None], (out_ref.shape[0],) + part.shape)


def add_kernel(parts_any, out_ref, parts_ref):
    pltpu.sync_copy(parts_any, parts_ref)
    out_ref[...] = jnp.sum(parts_ref[...].astype(F32), axis=0).astype(out_ref.dtype)


def local(queries, res_cache, res_count, move_cache, move_request, move_owner, out_weight):
    kv_size, tp_size = lax.axis_size("kv"), lax.axis_size("tp")
    owners = move_owner.reshape(-1)
    parts = pl.pallas_call(
        attend_kernel,
        out_shape=jax.ShapeDtypeStruct((kv_size, 16, HD), BF16),
        in_specs=[VMEM, VMEM, VMEM, SMEM, SMEM, VMEM, VMEM],
        out_specs=VMEM,
        name="attend",
    )(queries, res_cache, move_cache, res_count, move_request, owners[None, :], move_request[None, :])
    page = move_cache.shape[1:]

    def pages(n):
        return jax.ShapeDtypeStruct((n,) + page, BF16)

    def shift(x, chips):
        pairs = [(i, (i + 2 * chips * (1 - 2 * (i % 2))) % kv_size) for i in range(kv_size)]
        return lax.ppermute(x, "kv", pairs)

    def swap(x):
        return lax.ppermute(x, "kv", [(i, i ^ 1) for i in range(kv_size)])

    own, other = pl.pallas_call(
        pack_kernel,
        out_shape=(pages(HOME + CAP), pages(GIVEN + CAP)),
        in_specs=[VMEM, SMEM, ANY],
        out_specs=(VMEM, VMEM),
        scratch_shapes=[pltpu.SMEM((kv_size,), jnp.int32)],
        name="pack",
    )(move_cache, owners, parts)
    got = swap(other)
    parts = lax.all_to_all(parts, "kv", split_axis=0, concat_axis=0, tiled=True)
    def copies(kernel, name, out_pages, count, *args, out=ANY):
        return pl.pallas_call(
            kernel,
            out_shape=tuple(pages(n) for n in out_pages),
            in_specs=[ANY] * len(args),
            out_specs=(out,) * len(out_pages),
            scratch_shapes=[pltpu.SemaphoreType.DMA((count,))],
            compiler_params=pltpu.CompilerParams(vmem_limit_bytes=SMALL),
            cost_estimate=pl.CostEstimate(flops=0, bytes_accessed=1024, transcendentals=0),
            name=name,
        )(*args)

    (six,) = copies(merge_six_kernel, "merge_six", (5 * QUAD,), 2, own, got)
    (three,) = copies(merge_three_kernel, "merge_three", (6 * QUAD,), 2, own, got, six)
    part, landed_ids = pl.pallas_call(
        column_kernel,
        out_shape=(
            jax.ShapeDtypeStruct((tp_size, 16, HD), BF16),
            jax.ShapeDtypeStruct((1, kv_size * CAP), jnp.int32),
        ),
        in_specs=[ANY, ANY],
        out_specs=(VMEM, VMEM),
        scratch_shapes=[pltpu.VMEM(parts.shape, BF16)],
        compiler_params=pltpu.CompilerParams(vmem_limit_bytes=SMALL),
        name="column",
        cost_estimate=pl.CostEstimate(flops=0, bytes_accessed=1024, transcendentals=0),
    )(parts, three)
    six, three = shift(six, 6), shift(three, 3)
    columns = lax.all_to_all(part, "tp", split_axis=0, concat_axis=0, tiled=True)
    half = out_weight.shape[1] // 2
    partial_out = pl.pallas_call(
        project_kernel,
        out_shape=jax.ShapeDtypeStruct((CHIPS, 2, B, half), BF16),
        in_specs=[ANY, VMEM],
        out_specs=VMEM,
        scratch_shapes=[pltpu.VMEM(columns.shape, BF16)],
        compiler_params=pltpu.CompilerParams(vmem_limit_bytes=SMALL),
        name="project",
        cost_estimate=pl.CostEstimate(flops=0, bytes_accessed=1024, transcendentals=0),
    )(columns, out_weight)
    partials = lax.all_to_all(
        partial_out.reshape(kv_size, B, half), "kv", split_axis=0, concat_axis=0, tiled=True
    )
    mixed_half = pl.pallas_call(
        add_kernel,
        out_shape=jax.ShapeDtypeStruct((B, half), BF16),
        in_specs=[ANY],
        out_specs=VMEM,
        scratch_shapes=[pltpu.VMEM(partials.shape, BF16)],
        compiler_params=pltpu.CompilerParams(vmem_limit_bytes=SMALL),
        name="add",
        cost_estimate=pl.CostEstimate(flops=0, bytes_accessed=1024, transcendentals=0),
    )(partials)
    both_cores = [[2 * z, 2 * z + 1] for z in range(CHIPS)]
    mixed = lax.all_gather(mixed_half, "kv", axis=1, tiled=True, axis_index_groups=both_cores)
    one, two = copies(forward_kernel, "forward", (6 * QUAD, 5 * QUAD), 11, own, got, three, six, partial_out)
    two, one = shift(two, 2), shift(one, 1)
    (give,) = copies(give_kernel, "give", (GIVEN + CAP,), 15, three, six, one, two, mixed_half)
    taken = swap(give)
    (landed,) = copies(land_kernel, "land", (kv_size * CAP,), 25, own, got, three, six, one, two, taken, out=VMEM)
    return (mixed, landed, landed_ids.reshape(-1))


def solution(mesh):
    placed = (
        P(),
        P(("kv", "tp"), None, None, None),
        P(("kv", "tp"), None),
        P(("kv", "tp"), None, None, None),
        P(("kv", "tp")),
        P(("kv", "tp"), None),
        P("kv", "tp"),
    )
    return jax.shard_map(
        local,
        mesh=mesh,
        in_specs=placed,
        out_specs=(P(None, "tp"), P(("kv", "tp"), None, None, None), P(("kv", "tp"))),
        check_vma=False,
    )
```

```python
import math

import jax
import jax.numpy as jnp
from jax import lax
from jax.experimental import pallas as pl
from jax.experimental.pallas import tpu as pltpu
from jax.sharding import PartitionSpec as P

HQ = 64
KVH = 4
HD = 128
GROUP = 16
B = 4
PAGE = 8
CAP = 2
CHIPS = 16
NEG = -1e30
SMALL = 8 * 2**20

VMEM = pl.BlockSpec(memory_space=pltpu.VMEM)
ANY = pl.BlockSpec(memory_space=pl.ANY)
SMEM = pl.BlockSpec(memory_space=pltpu.SMEM)
F32 = jnp.float32
BF16 = jnp.bfloat16


def iota(shape, dim):
    return lax.broadcasted_iota(jnp.int32, shape, dim)


def round_up(x):
    return (x + jnp.abs(x) * 2.0**-7).astype(BF16).astype(F32)


def token_rows(ref, part):
    pages = ref[:, part].astype(F32)
    return pages.reshape(pages.shape[0] * PAGE, KVH * HD).astype(BF16)


def side_lanes(lane, shift, weight_sum):
    high = weight_sum.astype(BF16).astype(F32)
    return jnp.where(lane == 0, shift, jnp.where(lane == 1, high, jnp.where(lane == 4, weight_sum - high, 0.0)))


def attend_kernel(q_ref, res_ref, move_ref, count_ref, request_ref, owner_ref, request_row_ref, after_ref, out_ref):
    del after_ref
    rows = GROUP * B
    n_res, n_move = res_ref.shape[0], move_ref.shape[0]
    page = iota((8, n_res * PAGE), 1) // PAGE
    end = jnp.int32(0)
    res_request = jnp.zeros_like(page)
    for b in range(B - 1):
        end = end + count_ref[0, b]
        res_request = res_request + (page >= end).astype(jnp.int32)
    page = iota((8, n_move * PAGE), 1) // PAGE
    move_request = jnp.zeros_like(page)
    for p in range(n_move):
        move_request = jnp.where(page == p, request_ref[p], move_request)
    token_request = jnp.concatenate([res_request, move_request], axis=1)
    wanted = iota((8, token_request.shape[1]), 0) % B == token_request
    wanted = jnp.concatenate([wanted.astype(F32)] * (rows // 8), axis=0) > 0.5

    keys = jnp.concatenate([token_rows(res_ref, 0), token_rows(move_ref, 0)], axis=0)
    values = jnp.concatenate([token_rows(res_ref, 1), token_rows(move_ref, 1)], axis=0)
    q = q_ref[...].astype(F32)

    owner = owner_ref[...]
    column = jnp.sum(
        jnp.where(iota((n_move, n_move), 0) == iota((n_move, n_move), 1), owner, 0), axis=1, keepdims=True
    )
    before = (column == owner) & (iota((n_move, n_move), 0) < iota((n_move, n_move), 1))
    rank = jnp.sum(before.astype(jnp.int32), axis=0, keepdims=True)
    all_rows = out_ref.shape[0] * 8
    named = iota((all_rows, n_move), 0) // 8 == owner
    marks = request_row_ref[...] + 1
    slot_ids = [
        (jnp.sum(jnp.where(named & (rank == r), marks, 0), axis=1, keepdims=True) - 1).astype(F32)
        for r in range(CAP)
    ]

    lane = iota((rows, HD), 1)
    per = rows // 8
    for g in range(KVH):
        heads = [q[:, (g * GROUP + i) * HD : (g * GROUP + i + 1) * HD] for i in range(GROUP)]
        q_rows = jnp.concatenate(heads, axis=0).astype(BF16)
        scores = lax.dot_general(
            q_rows, keys[:, g * HD : (g + 1) * HD], (((1,), (1,)), ((), ())), preferred_element_type=F32
        ) * (1.0 / math.sqrt(HD))
        scores = jnp.where(wanted, scores, NEG)
        shift = round_up(jnp.max(scores, axis=1, keepdims=True))
        weights = jnp.where(wanted, jnp.exp(scores - shift), 0.0).astype(BF16)
        weight_sum = jnp.sum(weights.astype(F32), axis=1, keepdims=True)
        summed = jnp.dot(weights, values[:, g * HD : (g + 1) * HD], preferred_element_type=F32)
        own = slice(g * rows, (g + 1) * rows)
        extra = side_lanes(lane, shift, weight_sum)
        for r in range(CAP):
            extra = jnp.where(lane == 2 + r, slot_ids[r][own], extra)
        both = jnp.concatenate([summed.reshape(per, 8, HD), extra.reshape(per, 8, HD)], axis=1)
        out_ref[g * per : (g + 1) * per] = both.astype(BF16)


FAR = 8
QUAD = 4
HOME = QUAD * FAR
GIVEN = QUAD * (FAR - 1)


def copy_all(copies, sems):
    running = [pltpu.make_async_copy(a, b, sems.at[n]) for n, (a, b) in enumerate(copies)]
    for copy in running:
        copy.start()
    for copy in running:
        copy.wait()


def quads(ref, first, count=1):
    return ref.at[pl.ds(first * QUAD, count * QUAD)]


def pack_kernel(move_ref, owner_ref, own_ref, other_ref, used_ref):
    own_ref[...] = jnp.zeros(own_ref.shape, own_ref.dtype)
    other_ref[...] = jnp.zeros(other_ref.shape, other_ref.dtype)
    for o in range(used_ref.shape[0]):
        used_ref[o] = 0
    me = lax.axis_index("kv")
    chip, core = me // 2, me % 2

    def place(p, carry):
        owner = owner_ref[p]
        rank = used_ref[owner]
        used_ref[owner] = rank + 1
        up = (owner // 2 - chip) & (CHIPS - 1)
        lands = owner % 2
        carrier = jnp.where(up == 0, lands, jnp.where(up == FAR, core, (up > FAR).astype(jnp.int32)))
        distance = jnp.where(up > FAR, CHIPS - up, up)
        slot = (distance - 1) * 4 + jnp.where(lands == carrier, 0, CAP) + rank
        home = jnp.where(carrier == core, HOME, GIVEN) + rank
        slot = jnp.where(up == 0, home, slot)

        @pl.when(carrier == core)
        def _():
            own_ref[slot] = move_ref[p]

        @pl.when(carrier != core)
        def _():
            other_ref[slot] = move_ref[p]

        return carry

    lax.fori_loop(0, move_ref.shape[0], place, 0)


def merge_six_kernel(own_ref, got_ref, out_ref, sems):
    pairs = [(quads(own_ref, 5, 3), quads(out_ref, 0, 3)), (quads(got_ref, 5, 2), quads(out_ref, 3, 2))]
    copy_all(pairs, sems)


def merge_three_kernel(own_ref, got_ref, after_ref, out_ref, sems):
    del after_ref
    pairs = [(quads(own_ref, 2, 3), quads(out_ref, 0, 3)), (quads(got_ref, 2, 3), quads(out_ref, 3, 3))]
    copy_all(pairs, sems)


def forward_kernel(own_ref, got_ref, three_ref, six_ref, after_ref, one_ref, two_ref, sems):
    del after_ref
    copies = []
    for n, ref in enumerate((one_ref, two_ref)):
        parts = [(own_ref, n), (got_ref, n), (three_ref, 1 + n), (three_ref, 4 + n), (six_ref, 1 + n)]
        parts += [(six_ref, 4)] if n == 0 else []
        copies += [(quads(source, first), quads(ref, to)) for to, (source, first) in enumerate(parts)]
    copy_all(copies, sems)


def arrived(three_ref, six_ref, one_ref, two_ref):
    return (
        (1, one_ref, 0, 1),
        (2, two_ref, 0, 1),
        (3, three_ref, 0, 3),
        (4, one_ref, 2, 3),
        (5, two_ref, 2, 3),
        (6, six_ref, 0, 3),
        (7, one_ref, 4, 5),
    )


def give_kernel(three_ref, six_ref, one_ref, two_ref, after_ref, out_ref, sems):
    del after_ref
    core = lax.axis_index("kv") % 2
    copies = [(two_ref.at[pl.ds(4 * QUAD + CAP, CAP)], out_ref.at[pl.ds(GIVEN, CAP)])]
    for distance, ref, same, other in arrived(three_ref, six_ref, one_ref, two_ref):
        for quad, start in ((same, core), (other, 1 - core)):
            to = out_ref.at[pl.ds((distance - 1) * QUAD + start * CAP, CAP)]
            copies.append((ref.at[pl.ds(quad * QUAD + CAP, CAP)], to))
    copy_all(copies, sems)


def land_kernel(own_ref, got_ref, three_ref, six_ref, one_ref, two_ref, taken_ref, out_ref, sems):
    me = lax.axis_index("kv")
    chip, core = me // 2, me % 2
    way = 1 - 2 * core

    def rows(up, start):
        return out_ref.at[pl.ds(((chip + up) & (CHIPS - 1)) * QUAD + start * CAP, CAP)]

    copies = [
        (own_ref.at[pl.ds(HOME, CAP)], rows(0, core)),
        (got_ref.at[pl.ds(GIVEN, CAP)], rows(0, 1 - core)),
        (two_ref.at[pl.ds(4 * QUAD, CAP)], rows(FAR, core)),
        (taken_ref.at[pl.ds(GIVEN, CAP)], rows(FAR, 1 - core)),
    ]
    for distance, ref, same, other in arrived(three_ref, six_ref, one_ref, two_ref):
        for quad, start in ((same, core), (other, 1 - core)):
            copies.append((ref.at[pl.ds(quad * QUAD, CAP)], rows(-way * distance, start)))
        to = out_ref.at[pl.ds(((chip + way * distance) & (CHIPS - 1)) * QUAD, QUAD)]
        copies.append((quads(taken_ref, distance - 1), to))
    copy_all(copies, sems)


def combined(parts):
    shifts, values = parts[:, 8:, 0:1], parts[:, :8, :]
    sums = parts[:, 8:, 1:2] + parts[:, 8:, 4:5]
    shift = jnp.max(shifts, axis=0)
    factor = jnp.exp(shifts - shift[None])
    return shift, jnp.sum(sums * factor, axis=0), jnp.sum(values * factor, axis=0)


def fill_kernel(after_ref, out_ref):
    del after_ref
    out_ref[...] = jnp.zeros(out_ref.shape, F32)


def column_kernel(parts_any, after_ref, fill_ref, out_ref, ids_ref, parts_ref):
    del after_ref, fill_ref
    pltpu.sync_copy(parts_any, parts_ref)
    parts = parts_ref[...].astype(F32)
    shift, weight_sum, values = combined(parts)
    lane = iota((8, HD), 1)
    extra = side_lanes(lane, shift, weight_sum)
    out = jnp.concatenate([values, extra], axis=0).astype(out_ref.dtype)
    out_ref[...] = jnp.broadcast_to(out[None], out_ref.shape)
    n = parts.shape[0]
    source, place = iota((n, n * CAP), 0), iota((n, n * CAP), 1)
    ids = parts[:, 8, :]
    ids = jnp.where(place % CAP == 0, ids[:, 2:3], ids[:, 3:4])
    ids_ref[...] = jnp.sum(jnp.where(source == place // CAP, ids, 0.0), axis=0, keepdims=True).astype(jnp.int32)


def project_kernel(parts_any, weight_ref, out_ref, parts_ref):
    pltpu.sync_copy(parts_any, parts_ref)
    _, weight_sum, values = combined(parts_ref[...].astype(F32))
    attended = (values / weight_sum).astype(BF16)
    upper = jnp.dot(attended, weight_ref[:HD], preferred_element_type=F32)
    lower = jnp.dot(attended, weight_ref[HD:], preferred_element_type=F32)
    partial = (upper[:B] + lower[B:]).astype(out_ref.dtype)
    half = partial.shape[1] // 2
    for core in range(2):
        part = partial[:, core * half : (core + 1) * half]
        out_ref[:, core] = jnp.broadcast_to(part[None], (out_ref.shape[0],) + part.shape)


def add_kernel(parts_any, out_ref, parts_ref):
    pltpu.sync_copy(parts_any, parts_ref)
    out_ref[...] = jnp.sum(parts_ref[...].astype(F32), axis=0).astype(out_ref.dtype)


def local(queries, res_cache, res_count, move_cache, move_request, move_owner, out_weight):
    kv_size, tp_size = lax.axis_size("kv"), lax.axis_size("tp")
    owners = move_owner.reshape(-1)
    page = move_cache.shape[1:]

    def pages(n):
        return jax.ShapeDtypeStruct((n,) + page, BF16)

    def shift(x, chips):
        pairs = [(i, (i + 2 * chips * (1 - 2 * (i % 2))) % kv_size) for i in range(kv_size)]
        return lax.ppermute(x, "kv", pairs)

    def swap(x):
        return lax.ppermute(x, "kv", [(i, i ^ 1) for i in range(kv_size)])

    own, other = pl.pallas_call(
        pack_kernel,
        out_shape=(pages(HOME + CAP), pages(GIVEN + CAP)),
        in_specs=[VMEM, SMEM],
        out_specs=(VMEM, VMEM),
        scratch_shapes=[pltpu.SMEM((kv_size,), jnp.int32)],
        name="pack",
    )(move_cache, owners)
    got = swap(other)
    def copies(kernel, name, out_pages, count, *args, out=ANY):
        return pl.pallas_call(
            kernel,
            out_shape=tuple(pages(n) for n in out_pages),
            in_specs=[ANY] * len(args),
            out_specs=(out,) * len(out_pages),
            scratch_shapes=[pltpu.SemaphoreType.DMA((count,))],
            compiler_params=pltpu.CompilerParams(vmem_limit_bytes=SMALL),
            cost_estimate=pl.CostEstimate(flops=0, bytes_accessed=1024, transcendentals=0),
            name=name,
        )(*args)

    (six,) = copies(merge_six_kernel, "merge_six", (5 * QUAD,), 2, own, got)
    six_up = shift(six, 6)
    parts = pl.pallas_call(
        attend_kernel,
        out_shape=jax.ShapeDtypeStruct((kv_size, 16, HD), BF16),
        in_specs=[VMEM, VMEM, VMEM, SMEM, SMEM, VMEM, VMEM, ANY],
        out_specs=VMEM,
        name="attend",
    )(queries, res_cache, move_cache, res_count, move_request, owners[None, :], move_request[None, :], six)
    (three,) = copies(merge_three_kernel, "merge_three", (6 * QUAD,), 2, own, got, parts)
    three_up = shift(three, 3)
    parts = lax.all_to_all(parts, "kv", split_axis=0, concat_axis=0, tiled=True)
    fill = pl.pallas_call(
        fill_kernel,
        out_shape=jax.ShapeDtypeStruct((8, 128), F32),
        in_specs=[ANY],
        out_specs=VMEM,
        cost_estimate=pl.CostEstimate(flops=100000000000, bytes_accessed=1000000, transcendentals=0),
        name="fill",
    )(res_count)
    part, landed_ids = pl.pallas_call(
        column_kernel,
        out_shape=(
            jax.ShapeDtypeStruct((tp_size, 16, HD), BF16),
            jax.ShapeDtypeStruct((1, kv_size * CAP), jnp.int32),
        ),
        in_specs=[ANY, ANY, ANY],
        out_specs=(VMEM, VMEM),
        scratch_shapes=[pltpu.VMEM(parts.shape, BF16)],
        compiler_params=pltpu.CompilerParams(vmem_limit_bytes=SMALL),
        name="column",
        cost_estimate=pl.CostEstimate(flops=0, bytes_accessed=1024, transcendentals=0),
    )(parts, three, fill)
    six, three = six_up, three_up
    columns = lax.all_to_all(part, "tp", split_axis=0, concat_axis=0, tiled=True)
    half = out_weight.shape[1] // 2
    partial_out = pl.pallas_call(
        project_kernel,
        out_shape=jax.ShapeDtypeStruct((CHIPS, 2, B, half), BF16),
        in_specs=[ANY, VMEM],
        out_specs=VMEM,
        scratch_shapes=[pltpu.VMEM(columns.shape, BF16)],
        compiler_params=pltpu.CompilerParams(vmem_limit_bytes=SMALL),
        name="project",
        cost_estimate=pl.CostEstimate(flops=0, bytes_accessed=1024, transcendentals=0),
    )(columns, out_weight)
    partials = lax.all_to_all(
        partial_out.reshape(kv_size, B, half), "kv", split_axis=0, concat_axis=0, tiled=True
    )
    mixed_half = pl.pallas_call(
        add_kernel,
        out_shape=jax.ShapeDtypeStruct((B, half), BF16),
        in_specs=[ANY],
        out_specs=VMEM,
        scratch_shapes=[pltpu.VMEM(partials.shape, BF16)],
        compiler_params=pltpu.CompilerParams(vmem_limit_bytes=SMALL),
        name="add",
        cost_estimate=pl.CostEstimate(flops=0, bytes_accessed=1024, transcendentals=0),
    )(partials)
    both_cores = [[2 * z, 2 * z + 1] for z in range(CHIPS)]
    mixed = lax.all_gather(mixed_half, "kv", axis=1, tiled=True, axis_index_groups=both_cores)
    one, two = copies(forward_kernel, "forward", (6 * QUAD, 5 * QUAD), 11, own, got, three, six, partial_out)
    two, one = shift(two, 2), shift(one, 1)
    (give,) = copies(give_kernel, "give", (GIVEN + CAP,), 15, three, six, one, two, mixed_half)
    taken = swap(give)
    (landed,) = copies(land_kernel, "land", (kv_size * CAP,), 25, own, got, three, six, one, two, taken, out=VMEM)
    return (mixed, landed, landed_ids.reshape(-1))


def solution(mesh):
    placed = (
        P(),
        P(("kv", "tp"), None, None, None),
        P(("kv", "tp"), None),
        P(("kv", "tp"), None, None, None),
        P(("kv", "tp")),
        P(("kv", "tp"), None),
        P("kv", "tp"),
    )
    return jax.shard_map(
        local,
        mesh=mesh,
        in_specs=placed,
        out_specs=(P(None, "tp"), P(("kv", "tp"), None, None, None), P(("kv", "tp"))),
        check_vma=False,
    )
```

```python
import math

import jax
import jax.numpy as jnp
from jax import lax
from jax.experimental import pallas as pl
from jax.experimental.pallas import tpu as pltpu
from jax.sharding import PartitionSpec as P

HQ = 64
KVH = 4
HD = 128
GROUP = 16
B = 4
PAGE = 8
CAP = 2
CHIPS = 16
NEG = -1e30
SMALL = 8 * 2**20

VMEM = pl.BlockSpec(memory_space=pltpu.VMEM)
ANY = pl.BlockSpec(memory_space=pl.ANY)
SMEM = pl.BlockSpec(memory_space=pltpu.SMEM)
F32 = jnp.float32
BF16 = jnp.bfloat16


def iota(shape, dim):
    return lax.broadcasted_iota(jnp.int32, shape, dim)


def round_up(x):
    return (x + jnp.abs(x) * 2.0**-7).astype(BF16).astype(F32)


def token_rows(ref, part):
    pages = ref[:, part].astype(F32)
    return pages.reshape(pages.shape[0] * PAGE, KVH * HD).astype(BF16)


def side_lanes(lane, shift, weight_sum):
    high = weight_sum.astype(BF16).astype(F32)
    return jnp.where(lane == 0, shift, jnp.where(lane == 1, high, jnp.where(lane == 4, weight_sum - high, 0.0)))


def attend_kernel(q_ref, res_ref, move_ref, count_ref, request_ref, owner_ref, request_row_ref, out_ref):
    rows = GROUP * B
    n_res, n_move = res_ref.shape[0], move_ref.shape[0]
    page = iota((8, n_res * PAGE), 1) // PAGE
    end = jnp.int32(0)
    res_request = jnp.zeros_like(page)
    for b in range(B - 1):
        end = end + count_ref[0, b]
        res_request = res_request + (page >= end).astype(jnp.int32)
    page = iota((8, n_move * PAGE), 1) // PAGE
    move_request = jnp.zeros_like(page)
    for p in range(n_move):
        move_request = jnp.where(page == p, request_ref[p], move_request)
    token_request = jnp.concatenate([res_request, move_request], axis=1)
    wanted = iota((8, token_request.shape[1]), 0) % B == token_request
    wanted = jnp.concatenate([wanted.astype(F32)] * (rows // 8), axis=0) > 0.5

    keys = jnp.concatenate([token_rows(res_ref, 0), token_rows(move_ref, 0)], axis=0)
    values = jnp.concatenate([token_rows(res_ref, 1), token_rows(move_ref, 1)], axis=0)
    q = q_ref[...].astype(F32)

    owner = owner_ref[...]
    column = jnp.sum(
        jnp.where(iota((n_move, n_move), 0) == iota((n_move, n_move), 1), owner, 0), axis=1, keepdims=True
    )
    before = (column == owner) & (iota((n_move, n_move), 0) < iota((n_move, n_move), 1))
    rank = jnp.sum(before.astype(jnp.int32), axis=0, keepdims=True)
    all_rows = out_ref.shape[0] * 8
    named = iota((all_rows, n_move), 0) // 8 == owner
    marks = request_row_ref[...] + 1
    slot_ids = [
        (jnp.sum(jnp.where(named & (rank == r), marks, 0), axis=1, keepdims=True) - 1).astype(F32)
        for r in range(CAP)
    ]

    lane = iota((rows, HD), 1)
    per = rows // 8
    for g in range(KVH):
        heads = [q[:, (g * GROUP + i) * HD : (g * GROUP + i + 1) * HD] for i in range(GROUP)]
        q_rows = jnp.concatenate(heads, axis=0).astype(BF16)
        scores = lax.dot_general(
            q_rows, keys[:, g * HD : (g + 1) * HD], (((1,), (1,)), ((), ())), preferred_element_type=F32
        ) * (1.0 / math.sqrt(HD))
        scores = jnp.where(wanted, scores, NEG)
        shift = round_up(jnp.max(scores, axis=1, keepdims=True))
        weights = jnp.where(wanted, jnp.exp(scores - shift), 0.0).astype(BF16)
        weight_sum = jnp.sum(weights.astype(F32), axis=1, keepdims=True)
        summed = jnp.dot(weights, values[:, g * HD : (g + 1) * HD], preferred_element_type=F32)
        own = slice(g * rows, (g + 1) * rows)
        extra = side_lanes(lane, shift, weight_sum)
        for r in range(CAP):
            extra = jnp.where(lane == 2 + r, slot_ids[r][own], extra)
        both = jnp.concatenate([summed.reshape(per, 8, HD), extra.reshape(per, 8, HD)], axis=1)
        out_ref[g * per : (g + 1) * per] = both.astype(BF16)


FAR = 8
QUAD = 4
HOME = QUAD * FAR
GIVEN = QUAD * (FAR - 1)


def copy_all(copies, sems):
    running = [pltpu.make_async_copy(a, b, sems.at[n]) for n, (a, b) in enumerate(copies)]
    for copy in running:
        copy.start()
    for copy in running:
        copy.wait()


def quads(ref, first, count=1):
    return ref.at[pl.ds(first * QUAD, count * QUAD)]


def pack_kernel(move_ref, owner_ref, own_out, other_out, own_ref, other_ref, used_ref, sems):
    own_ref[...] = jnp.zeros(own_ref.shape, own_ref.dtype)
    other_ref[...] = jnp.zeros(other_ref.shape, other_ref.dtype)
    for o in range(used_ref.shape[0]):
        used_ref[o] = 0
    me = lax.axis_index("kv")
    chip, core = me // 2, me % 2

    def place(p, carry):
        owner = owner_ref[p]
        rank = used_ref[owner]
        used_ref[owner] = rank + 1
        up = (owner // 2 - chip) & (CHIPS - 1)
        lands = owner % 2
        carrier = jnp.where(up == 0, lands, jnp.where(up == FAR, core, (up > FAR).astype(jnp.int32)))
        distance = jnp.where(up > FAR, CHIPS - up, up)
        slot = (distance - 1) * 4 + jnp.where(lands == carrier, 0, CAP) + rank
        home = jnp.where(carrier == core, HOME, GIVEN) + rank
        slot = jnp.where(up == 0, home, slot)

        @pl.when(carrier == core)
        def _():
            own_ref[slot] = move_ref[p]

        @pl.when(carrier != core)
        def _():
            other_ref[slot] = move_ref[p]

        return carry

    lax.fori_loop(0, move_ref.shape[0], place, 0)
    copy_all([(own_ref, own_out), (other_ref, other_out)], sems)


def short_kernel(own_ref, got_ref, after_ref, one_ref, two_ref, sems):
    del after_ref
    copies = []
    for n, ref in enumerate((one_ref, two_ref)):
        for m in range(3):
            copies.append((quads(own_ref, n + 3 * m), quads(ref, 2 * m)))
            if n + 3 * m < FAR - 1:
                copies.append((quads(got_ref, n + 3 * m), quads(ref, 2 * m + 1)))
    copy_all(copies, sems)


def long_kernel(own_ref, got_ref, one_ref, two_ref, three_ref, six_ref, sems):
    copies = []
    for n, ref in enumerate((three_ref, six_ref)):
        own = 2 + 3 * n
        copies += [(quads(own_ref, own), quads(ref, 0)), (quads(got_ref, own), quads(ref, 1))]
        copies.append((quads(one_ref, 2 + 2 * n, 2), quads(ref, 2, 2)))
        count = 2 - n
        copies.append((quads(two_ref, 2 + 2 * n, count), quads(ref, 4, count)))
    copy_all(copies, sems)


def arrived(one_ref, two_ref, three_ref, six_ref):
    return (
        (1, one_ref, 0),
        (2, two_ref, 0),
        (3, three_ref, 0),
        (4, three_ref, 2),
        (5, three_ref, 4),
        (6, six_ref, 0),
        (7, six_ref, 2),
    )


def give_kernel(one_ref, two_ref, three_ref, six_ref, out_ref, sems):
    core = lax.axis_index("kv") % 2
    copies = [(six_ref.at[pl.ds(4 * QUAD + CAP, CAP)], out_ref.at[pl.ds(GIVEN, CAP)])]
    for distance, ref, quad in arrived(one_ref, two_ref, three_ref, six_ref):
        for quad, start in ((quad, core), (quad + 1, 1 - core)):
            to = out_ref.at[pl.ds((distance - 1) * QUAD + start * CAP, CAP)]
            copies.append((ref.at[pl.ds(quad * QUAD + CAP, CAP)], to))
    copy_all(copies, sems)


def land_kernel(own_ref, got_ref, one_ref, two_ref, three_ref, six_ref, taken_ref, out_ref, passed_ref, sems):
    me = lax.axis_index("kv")
    chip, core = me // 2, me % 2
    way = 1 - 2 * core

    def rows(up, start):
        return out_ref.at[pl.ds(((chip + up) & (CHIPS - 1)) * QUAD + start * CAP, CAP)]

    copies = [
        (own_ref.at[pl.ds(HOME, CAP)], rows(0, core)),
        (got_ref.at[pl.ds(GIVEN, CAP)], rows(0, 1 - core)),
        (six_ref.at[pl.ds(4 * QUAD, CAP)], rows(FAR, core)),
        (taken_ref.at[pl.ds(GIVEN, CAP)], rows(FAR, 1 - core)),
    ]
    for distance, ref, quad in arrived(one_ref, two_ref, three_ref, six_ref):
        for quad, start in ((quad, core), (quad + 1, 1 - core)):
            copies.append((ref.at[pl.ds(quad * QUAD, CAP)], rows(-way * distance, start)))
        to = out_ref.at[pl.ds(((chip + way * distance) & (CHIPS - 1)) * QUAD, QUAD)]
        copies.append((quads(taken_ref, distance - 1), to))
    copy_all(copies, sems)


def combined(parts):
    shifts, values = parts[:, 8:, 0:1], parts[:, :8, :]
    sums = parts[:, 8:, 1:2] + parts[:, 8:, 4:5]
    shift = jnp.max(shifts, axis=0)
    factor = jnp.exp(shifts - shift[None])
    return shift, jnp.sum(sums * factor, axis=0), jnp.sum(values * factor, axis=0)


def fill_kernel(*refs):
    del refs


def column_kernel(parts_any, after_ref, out_ref, ids_ref, parts_ref):
    del after_ref
    pltpu.sync_copy(parts_any, parts_ref)
    parts = parts_ref[...].astype(F32)
    shift, weight_sum, values = combined(parts)
    lane = iota((8, HD), 1)
    extra = side_lanes(lane, shift, weight_sum)
    out = jnp.concatenate([values, extra], axis=0).astype(out_ref.dtype)
    out_ref[...] = jnp.broadcast_to(out[None], out_ref.shape)
    n = parts.shape[0]
    source, place = iota((n, n * CAP), 0), iota((n, n * CAP), 1)
    ids = parts[:, 8, :]
    ids = jnp.where(place % CAP == 0, ids[:, 2:3], ids[:, 3:4])
    ids_ref[...] = jnp.sum(jnp.where(source == place // CAP, ids, 0.0), axis=0, keepdims=True).astype(jnp.int32)


def project_kernel(parts_any, weight_ref, out_ref, parts_ref):
    pltpu.sync_copy(parts_any, parts_ref)
    _, weight_sum, values = combined(parts_ref[...].astype(F32))
    attended = (values / weight_sum).astype(BF16)
    upper = jnp.dot(attended, weight_ref[:HD], preferred_element_type=F32)
    lower = jnp.dot(attended, weight_ref[HD:], preferred_element_type=F32)
    partial = (upper[:B] + lower[B:]).astype(out_ref.dtype)
    half = partial.shape[1] // 2
    for core in range(2):
        part = partial[:, core * half : (core + 1) * half]
        out_ref[:, core] = jnp.broadcast_to(part[None], (out_ref.shape[0],) + part.shape)


def add_kernel(parts_any, after_ref, out_ref, parts_ref):
    del after_ref
    pltpu.sync_copy(parts_any, parts_ref)
    out_ref[...] = jnp.sum(parts_ref[...].astype(F32), axis=0).astype(out_ref.dtype)


def local(queries, res_cache, res_count, move_cache, move_request, move_owner, out_weight):
    kv_size, tp_size = lax.axis_size("kv"), lax.axis_size("tp")
    owners = move_owner.reshape(-1)
    page = move_cache.shape[1:]

    def pages(n):
        return jax.ShapeDtypeStruct((n,) + page, BF16)

    def shift(x, chips):
        pairs = [(i, (i + 2 * chips * (1 - 2 * (i % 2))) % kv_size) for i in range(kv_size)]
        return lax.ppermute(x, "kv", pairs)

    def swap(x):
        return lax.ppermute(x, "kv", [(i, i ^ 1) for i in range(kv_size)])

    own, other = pl.pallas_call(
        pack_kernel,
        out_shape=(pages(HOME + CAP), pages(GIVEN + CAP)),
        in_specs=[VMEM, SMEM],
        out_specs=(ANY, ANY),
        scratch_shapes=[
            pltpu.VMEM((HOME + CAP,) + page, BF16),
            pltpu.VMEM((GIVEN + CAP,) + page, BF16),
            pltpu.SMEM((kv_size,), jnp.int32),
            pltpu.SemaphoreType.DMA((2,)),
        ],
        compiler_params=pltpu.CompilerParams(vmem_limit_bytes=SMALL),
        name="pack",
    )(move_cache, owners)
    got = swap(other)
    def copies(kernel, name, out_pages, count, *args):
        return pl.pallas_call(
            kernel,
            out_shape=tuple(pages(n) for n in out_pages),
            in_specs=[ANY] * len(args),
            out_specs=(ANY,) * len(out_pages),
            scratch_shapes=[pltpu.SemaphoreType.DMA((count,))],
            compiler_params=pltpu.CompilerParams(vmem_limit_bytes=SMALL),
            cost_estimate=pl.CostEstimate(flops=0, bytes_accessed=1024, transcendentals=0),
            name=name,
        )(*args)

    parts = pl.pallas_call(
        attend_kernel,
        out_shape=jax.ShapeDtypeStruct((kv_size, 16, HD), BF16),
        in_specs=[VMEM, VMEM, VMEM, SMEM, SMEM, VMEM, VMEM],
        out_specs=VMEM,
        name="attend",
    )(queries, res_cache, move_cache, res_count, move_request, owners[None, :], move_request[None, :])
    one, two = copies(short_kernel, "short", (6 * QUAD, 5 * QUAD), 11, own, got, parts)
    one, two = shift(one, 1), shift(two, 2)
    parts = lax.all_to_all(parts, "kv", split_axis=0, concat_axis=0, tiled=True)
    three, six = copies(long_kernel, "long", (6 * QUAD, 5 * QUAD), 8, own, got, one, two)
    six_up, three_up = shift(six, 6), shift(three, 3)
    own = pl.pallas_call(
        fill_kernel,
        out_shape=pages(HOME + CAP),
        in_specs=[ANY],
        out_specs=ANY,
        input_output_aliases={0: 0},
        compiler_params=pltpu.CompilerParams(vmem_limit_bytes=SMALL),
        cost_estimate=pl.CostEstimate(flops=10**11, bytes_accessed=1024, transcendentals=0),
        name="fill",
    )(own)
    part, landed_ids = pl.pallas_call(
        column_kernel,
        out_shape=(
            jax.ShapeDtypeStruct((tp_size, 16, HD), BF16),
            jax.ShapeDtypeStruct((1, kv_size * CAP), jnp.int32),
        ),
        in_specs=[ANY, ANY],
        out_specs=(VMEM, VMEM),
        scratch_shapes=[pltpu.VMEM(parts.shape, BF16)],
        compiler_params=pltpu.CompilerParams(vmem_limit_bytes=SMALL),
        name="column",
        cost_estimate=pl.CostEstimate(flops=0, bytes_accessed=1024, transcendentals=0),
    )(parts, own)
    six, three = six_up, three_up
    columns = lax.all_to_all(part, "tp", split_axis=0, concat_axis=0, tiled=True)
    half = out_weight.shape[1] // 2
    partial_out = pl.pallas_call(
        project_kernel,
        out_shape=jax.ShapeDtypeStruct((CHIPS, 2, B, half), BF16),
        in_specs=[ANY, VMEM],
        out_specs=VMEM,
        scratch_shapes=[pltpu.VMEM(columns.shape, BF16)],
        compiler_params=pltpu.CompilerParams(vmem_limit_bytes=SMALL),
        name="project",
        cost_estimate=pl.CostEstimate(flops=0, bytes_accessed=1024, transcendentals=0),
    )(columns, out_weight)
    partials = lax.all_to_all(
        partial_out.reshape(kv_size, B, half), "kv", split_axis=0, concat_axis=0, tiled=True
    )
    (give,) = copies(give_kernel, "give", (GIVEN + CAP,), 15, one, two, three, six)
    taken = swap(give)
    landed, own = pl.pallas_call(
        land_kernel,
        out_shape=(pages(kv_size * CAP), pages(HOME + CAP)),
        in_specs=[ANY] * 7,
        out_specs=(VMEM, ANY),
        input_output_aliases={0: 1},
        scratch_shapes=[pltpu.SemaphoreType.DMA((25,))],
        compiler_params=pltpu.CompilerParams(vmem_limit_bytes=SMALL),
        cost_estimate=pl.CostEstimate(flops=0, bytes_accessed=1024, transcendentals=0),
        name="land",
    )(own, got, one, two, three, six, taken)
    mixed_half = pl.pallas_call(
        add_kernel,
        out_shape=jax.ShapeDtypeStruct((B, half), BF16),
        in_specs=[ANY, ANY],
        out_specs=VMEM,
        scratch_shapes=[pltpu.VMEM(partials.shape, BF16)],
        compiler_params=pltpu.CompilerParams(vmem_limit_bytes=SMALL),
        name="add",
        cost_estimate=pl.CostEstimate(flops=0, bytes_accessed=1024, transcendentals=0),
    )(partials, own)
    both_cores = [[2 * z, 2 * z + 1] for z in range(CHIPS)]
    mixed = lax.all_gather(mixed_half, "kv", axis=1, tiled=True, axis_index_groups=both_cores)
    return (mixed, landed, landed_ids.reshape(-1))


def solution(mesh):
    placed = (
        P(),
        P(("kv", "tp"), None, None, None),
        P(("kv", "tp"), None),
        P(("kv", "tp"), None, None, None),
        P(("kv", "tp")),
        P(("kv", "tp"), None),
        P("kv", "tp"),
    )
    return jax.shard_map(
        local,
        mesh=mesh,
        in_specs=placed,
        out_specs=(P(None, "tp"), P(("kv", "tp"), None, None, None), P(("kv", "tp"))),
        check_vma=False,
    )
```

```python
import math

import jax
import jax.numpy as jnp
from jax import lax
from jax.experimental import pallas as pl
from jax.experimental.pallas import tpu as pltpu
from jax.sharding import PartitionSpec as P

HQ = 64
KVH = 4
HD = 128
GROUP = 16
B = 4
PAGE = 8
CAP = 2
CHIPS = 16
NEG = -1e30
SMALL = 8 * 2**20
LARGE = 56 * 2**20

VMEM = pl.BlockSpec(memory_space=pltpu.VMEM)
ANY = pl.BlockSpec(memory_space=pl.ANY)
SMEM = pl.BlockSpec(memory_space=pltpu.SMEM)
F32 = jnp.float32
BF16 = jnp.bfloat16


def iota(shape, dim):
    return lax.broadcasted_iota(jnp.int32, shape, dim)


def round_up(x):
    return (x + jnp.abs(x) * 2.0**-7).astype(BF16).astype(F32)


def token_rows(ref, part):
    pages = ref[:, part].astype(F32)
    return pages.reshape(pages.shape[0] * PAGE, KVH * HD).astype(BF16)


def side_lanes(lane, shift, weight_sum):
    high = weight_sum.astype(BF16).astype(F32)
    return jnp.where(lane == 0, shift, jnp.where(lane == 1, high, jnp.where(lane == 4, weight_sum - high, 0.0)))


def attend_kernel(q_ref, res_ref, move_ref, count_ref, request_ref, owner_ref, request_row_ref, out_ref):
    rows = GROUP * B
    n_res, n_move = res_ref.shape[0], move_ref.shape[0]
    page = iota((8, n_res * PAGE), 1) // PAGE
    end = jnp.int32(0)
    res_request = jnp.zeros_like(page)
    for b in range(B - 1):
        end = end + count_ref[0, b]
        res_request = res_request + (page >= end).astype(jnp.int32)
    page = iota((8, n_move * PAGE), 1) // PAGE
    move_request = jnp.zeros_like(page)
    for p in range(n_move):
        move_request = jnp.where(page == p, request_ref[p], move_request)
    token_request = jnp.concatenate([res_request, move_request], axis=1)
    wanted = iota((8, token_request.shape[1]), 0) % B == token_request
    wanted = jnp.concatenate([wanted.astype(F32)] * (rows // 8), axis=0) > 0.5

    keys = jnp.concatenate([token_rows(res_ref, 0), token_rows(move_ref, 0)], axis=0)
    values = jnp.concatenate([token_rows(res_ref, 1), token_rows(move_ref, 1)], axis=0)
    q = q_ref[...].astype(F32)

    owner = owner_ref[...]
    column = jnp.sum(
        jnp.where(iota((n_move, n_move), 0) == iota((n_move, n_move), 1), owner, 0), axis=1, keepdims=True
    )
    before = (column == owner) & (iota((n_move, n_move), 0) < iota((n_move, n_move), 1))
    rank = jnp.sum(before.astype(jnp.int32), axis=0, keepdims=True)
    all_rows = out_ref.shape[0] * 8
    named = iota((all_rows, n_move), 0) // 8 == owner
    marks = request_row_ref[...] + 1
    slot_ids = [
        (jnp.sum(jnp.where(named & (rank == r), marks, 0), axis=1, keepdims=True) - 1).astype(F32)
        for r in range(CAP)
    ]

    lane = iota((rows, HD), 1)
    per = rows // 8
    for g in range(KVH):
        heads = [q[:, (g * GROUP + i) * HD : (g * GROUP + i + 1) * HD] for i in range(GROUP)]
        q_rows = jnp.concatenate(heads, axis=0).astype(BF16)
        scores = lax.dot_general(
            q_rows, keys[:, g * HD : (g + 1) * HD], (((1,), (1,)), ((), ())), preferred_element_type=F32
        ) * (1.0 / math.sqrt(HD))
        scores = jnp.where(wanted, scores, NEG)
        shift = round_up(jnp.max(scores, axis=1, keepdims=True))
        weights = jnp.where(wanted, jnp.exp(scores - shift), 0.0).astype(BF16)
        weight_sum = jnp.sum(weights.astype(F32), axis=1, keepdims=True)
        summed = jnp.dot(weights, values[:, g * HD : (g + 1) * HD], preferred_element_type=F32)
        own = slice(g * rows, (g + 1) * rows)
        extra = side_lanes(lane, shift, weight_sum)
        for r in range(CAP):
            extra = jnp.where(lane == 2 + r, slot_ids[r][own], extra)
        both = jnp.concatenate([summed.reshape(per, 8, HD), extra.reshape(per, 8, HD)], axis=1)
        out_ref[g * per : (g + 1) * per] = both.astype(BF16)


FAR = 8
QUAD = 4
HOME = QUAD * FAR
GIVEN = QUAD * (FAR - 1)


def copy_all(copies, sems):
    running = [pltpu.make_async_copy(a, b, sems.at[n]) for n, (a, b) in enumerate(copies)]
    for copy in running:
        copy.start()
    for copy in running:
        copy.wait()


def quads(ref, first, count=1):
    return ref.at[pl.ds(first * QUAD, count * QUAD)]


def pack_kernel(move_ref, owner_ref, own_out, other_out, own_ref, other_ref, used_ref, sems):
    own_ref[...] = jnp.zeros(own_ref.shape, own_ref.dtype)
    other_ref[...] = jnp.zeros(other_ref.shape, other_ref.dtype)
    for o in range(used_ref.shape[0]):
        used_ref[o] = 0
    me = lax.axis_index("kv")
    chip, core = me // 2, me % 2

    def place(p, carry):
        owner = owner_ref[p]
        rank = used_ref[owner]
        used_ref[owner] = rank + 1
        up = (owner // 2 - chip) & (CHIPS - 1)
        lands = owner % 2
        carrier = jnp.where(up == 0, lands, jnp.where(up == FAR, core, (up > FAR).astype(jnp.int32)))
        distance = jnp.where(up > FAR, CHIPS - up, up)
        slot = (distance - 1) * 4 + jnp.where(lands == carrier, 0, CAP) + rank
        home = jnp.where(carrier == core, HOME, GIVEN) + rank
        slot = jnp.where(up == 0, home, slot)

        @pl.when(carrier == core)
        def _():
            own_ref[slot] = move_ref[p]

        @pl.when(carrier != core)
        def _():
            other_ref[slot] = move_ref[p]

        return carry

    lax.fori_loop(0, move_ref.shape[0], place, 0)
    copy_all([(own_ref, own_out), (other_ref, other_out)], sems)


def short_kernel(own_ref, got_ref, after_ref, one_ref, two_ref, sems):
    del after_ref
    copies = []
    for n, ref in enumerate((one_ref, two_ref)):
        for m in range(3):
            copies.append((quads(own_ref, n + 3 * m), quads(ref, 2 * m)))
            if n + 3 * m < FAR - 1:
                copies.append((quads(got_ref, n + 3 * m), quads(ref, 2 * m + 1)))
    copy_all(copies, sems)


def long_kernel(own_ref, got_ref, one_ref, two_ref, three_ref, six_ref, sems):
    copies = []
    for n, ref in enumerate((three_ref, six_ref)):
        own = 2 + 3 * n
        copies += [(quads(own_ref, own), quads(ref, 0)), (quads(got_ref, own), quads(ref, 1))]
        copies.append((quads(one_ref, 2 + 2 * n, 2), quads(ref, 2, 2)))
        count = 2 - n
        copies.append((quads(two_ref, 2 + 2 * n, count), quads(ref, 4, count)))
    copy_all(copies, sems)


def arrived(one_ref, two_ref, three_ref, six_ref):
    return (
        (1, one_ref, 0),
        (2, two_ref, 0),
        (3, three_ref, 0),
        (4, three_ref, 2),
        (5, three_ref, 4),
        (6, six_ref, 0),
        (7, six_ref, 2),
    )


def give_kernel(one_ref, two_ref, three_ref, six_ref, out_ref, sems):
    core = lax.axis_index("kv") % 2
    copies = [(six_ref.at[pl.ds(4 * QUAD + CAP, CAP)], out_ref.at[pl.ds(GIVEN, CAP)])]
    for distance, ref, quad in arrived(one_ref, two_ref, three_ref, six_ref):
        for quad, start in ((quad, core), (quad + 1, 1 - core)):
            to = out_ref.at[pl.ds((distance - 1) * QUAD + start * CAP, CAP)]
            copies.append((ref.at[pl.ds(quad * QUAD + CAP, CAP)], to))
    copy_all(copies, sems)


def land_kernel(own_ref, got_ref, one_ref, two_ref, three_ref, six_ref, taken_ref, out_ref, passed_ref, sems):
    me = lax.axis_index("kv")
    chip, core = me // 2, me % 2
    way = 1 - 2 * core

    def rows(up, start):
        return out_ref.at[pl.ds(((chip + up) & (CHIPS - 1)) * QUAD + start * CAP, CAP)]

    copies = [
        (own_ref.at[pl.ds(HOME, CAP)], rows(0, core)),
        (got_ref.at[pl.ds(GIVEN, CAP)], rows(0, 1 - core)),
        (six_ref.at[pl.ds(4 * QUAD, CAP)], rows(FAR, core)),
        (taken_ref.at[pl.ds(GIVEN, CAP)], rows(FAR, 1 - core)),
    ]
    for distance, ref, quad in arrived(one_ref, two_ref, three_ref, six_ref):
        for quad, start in ((quad, core), (quad + 1, 1 - core)):
            copies.append((ref.at[pl.ds(quad * QUAD, CAP)], rows(-way * distance, start)))
        to = out_ref.at[pl.ds(((chip + way * distance) & (CHIPS - 1)) * QUAD, QUAD)]
        copies.append((quads(taken_ref, distance - 1), to))
    copy_all(copies, sems)


def combined(parts):
    shifts, values = parts[:, 8:, 0:1], parts[:, :8, :]
    sums = parts[:, 8:, 1:2] + parts[:, 8:, 4:5]
    shift = jnp.max(shifts, axis=0)
    factor = jnp.exp(shifts - shift[None])
    return shift, jnp.sum(sums * factor, axis=0), jnp.sum(values * factor, axis=0)


def fill_kernel(*refs):
    del refs


def column_kernel(parts_any, after_ref, out_ref, ids_ref, parts_ref):
    del after_ref
    pltpu.sync_copy(parts_any, parts_ref)
    parts = parts_ref[...].astype(F32)
    shift, weight_sum, values = combined(parts)
    lane = iota((8, HD), 1)
    extra = side_lanes(lane, shift, weight_sum)
    out = jnp.concatenate([values, extra], axis=0).astype(out_ref.dtype)
    out_ref[...] = jnp.broadcast_to(out[None], out_ref.shape)
    n = parts.shape[0]
    source, place = iota((n, n * CAP), 0), iota((n, n * CAP), 1)
    ids = parts[:, 8, :]
    ids = jnp.where(place % CAP == 0, ids[:, 2:3], ids[:, 3:4])
    ids_ref[...] = jnp.sum(jnp.where(source == place // CAP, ids, 0.0), axis=0, keepdims=True).astype(jnp.int32)


def project_kernel(parts_any, weight_ref, out_ref, parts_ref):
    pltpu.sync_copy(parts_any, parts_ref)
    _, weight_sum, values = combined(parts_ref[...].astype(F32))
    attended = (values / weight_sum).astype(BF16)
    upper = jnp.dot(attended, weight_ref[:HD], preferred_element_type=F32)
    lower = jnp.dot(attended, weight_ref[HD:], preferred_element_type=F32)
    partial = (upper[:B] + lower[B:]).astype(out_ref.dtype)
    half = partial.shape[1] // 2
    for core in range(2):
        part = partial[:, core * half : (core + 1) * half]
        out_ref[:, core] = jnp.broadcast_to(part[None], (out_ref.shape[0],) + part.shape)


def add_kernel(parts_any, after_ref, out_ref, parts_ref):
    del after_ref
    pltpu.sync_copy(parts_any, parts_ref)
    out_ref[...] = jnp.sum(parts_ref[...].astype(F32), axis=0).astype(out_ref.dtype)


def local(queries, res_cache, res_count, move_cache, move_request, move_owner, out_weight):
    kv_size, tp_size = lax.axis_size("kv"), lax.axis_size("tp")
    owners = move_owner.reshape(-1)
    page = move_cache.shape[1:]

    def pages(n):
        return jax.ShapeDtypeStruct((n,) + page, BF16)

    def shift(x, chips):
        pairs = [(i, (i + 2 * chips * (1 - 2 * (i % 2))) % kv_size) for i in range(kv_size)]
        return lax.ppermute(x, "kv", pairs)

    def swap(x):
        return lax.ppermute(x, "kv", [(i, i ^ 1) for i in range(kv_size)])

    own, other = pl.pallas_call(
        pack_kernel,
        out_shape=(pages(HOME + CAP), pages(GIVEN + CAP)),
        in_specs=[VMEM, SMEM],
        out_specs=(ANY, ANY),
        scratch_shapes=[
            pltpu.VMEM((HOME + CAP,) + page, BF16),
            pltpu.VMEM((GIVEN + CAP,) + page, BF16),
            pltpu.SMEM((kv_size,), jnp.int32),
            pltpu.SemaphoreType.DMA((2,)),
        ],
        compiler_params=pltpu.CompilerParams(vmem_limit_bytes=LARGE),
        name="pack",
    )(move_cache, owners)
    got = swap(other)
    def copies(kernel, name, out_pages, count, *args):
        return pl.pallas_call(
            kernel,
            out_shape=tuple(pages(n) for n in out_pages),
            in_specs=[ANY] * len(args),
            out_specs=(ANY,) * len(out_pages),
            scratch_shapes=[pltpu.SemaphoreType.DMA((count,))],
            compiler_params=pltpu.CompilerParams(vmem_limit_bytes=SMALL),
            cost_estimate=pl.CostEstimate(flops=0, bytes_accessed=1024, transcendentals=0),
            name=name,
        )(*args)

    parts = pl.pallas_call(
        attend_kernel,
        out_shape=jax.ShapeDtypeStruct((kv_size, 16, HD), BF16),
        in_specs=[VMEM, VMEM, VMEM, SMEM, SMEM, VMEM, VMEM],
        out_specs=VMEM,
        name="attend",
    )(queries, res_cache, move_cache, res_count, move_request, owners[None, :], move_request[None, :])
    one, two = copies(short_kernel, "short", (6 * QUAD, 5 * QUAD), 11, own, got, parts)
    one, two = shift(one, 1), shift(two, 2)
    parts = lax.all_to_all(parts, "kv", split_axis=0, concat_axis=0, tiled=True)
    three, six = copies(long_kernel, "long", (6 * QUAD, 5 * QUAD), 8, own, got, one, two)
    six_up, three_up = shift(six, 6), shift(three, 3)
    own = pl.pallas_call(
        fill_kernel,
        out_shape=pages(HOME + CAP),
        in_specs=[ANY],
        out_specs=ANY,
        input_output_aliases={0: 0},
        compiler_params=pltpu.CompilerParams(vmem_limit_bytes=SMALL),
        cost_estimate=pl.CostEstimate(flops=10**11, bytes_accessed=1024, transcendentals=0),
        name="fill",
    )(own)
    part, landed_ids = pl.pallas_call(
        column_kernel,
        out_shape=(
            jax.ShapeDtypeStruct((tp_size, 16, HD), BF16),
            jax.ShapeDtypeStruct((1, kv_size * CAP), jnp.int32),
        ),
        in_specs=[ANY, ANY],
        out_specs=(VMEM, VMEM),
        scratch_shapes=[pltpu.VMEM(parts.shape, BF16)],
        compiler_params=pltpu.CompilerParams(vmem_limit_bytes=SMALL),
        name="column",
        cost_estimate=pl.CostEstimate(flops=0, bytes_accessed=1024, transcendentals=0),
    )(parts, own)
    six, three = six_up, three_up
    columns = lax.all_to_all(part, "tp", split_axis=0, concat_axis=0, tiled=True)
    half = out_weight.shape[1] // 2
    partial_out = pl.pallas_call(
        project_kernel,
        out_shape=jax.ShapeDtypeStruct((CHIPS, 2, B, half), BF16),
        in_specs=[ANY, VMEM],
        out_specs=VMEM,
        scratch_shapes=[pltpu.VMEM(columns.shape, BF16)],
        compiler_params=pltpu.CompilerParams(vmem_limit_bytes=SMALL),
        name="project",
        cost_estimate=pl.CostEstimate(flops=0, bytes_accessed=1024, transcendentals=0),
    )(columns, out_weight)
    partials = lax.all_to_all(
        partial_out.reshape(kv_size, B, half), "kv", split_axis=0, concat_axis=0, tiled=True
    )
    (give,) = copies(give_kernel, "give", (GIVEN + CAP,), 15, one, two, three, six)
    taken = swap(give)
    landed, own = pl.pallas_call(
        land_kernel,
        out_shape=(pages(kv_size * CAP), pages(HOME + CAP)),
        in_specs=[ANY] * 7,
        out_specs=(ANY, ANY),
        input_output_aliases={0: 1},
        scratch_shapes=[pltpu.SemaphoreType.DMA((25,))],
        compiler_params=pltpu.CompilerParams(vmem_limit_bytes=SMALL),
        cost_estimate=pl.CostEstimate(flops=0, bytes_accessed=1024, transcendentals=0),
        name="land",
    )(own, got, one, two, three, six, taken)
    mixed_half = pl.pallas_call(
        add_kernel,
        out_shape=jax.ShapeDtypeStruct((B, half), BF16),
        in_specs=[ANY, ANY],
        out_specs=VMEM,
        scratch_shapes=[pltpu.VMEM(partials.shape, BF16)],
        compiler_params=pltpu.CompilerParams(vmem_limit_bytes=SMALL),
        name="add",
        cost_estimate=pl.CostEstimate(flops=0, bytes_accessed=1024, transcendentals=0),
    )(partials, own)
    both_cores = [[2 * z, 2 * z + 1] for z in range(CHIPS)]
    mixed = lax.all_gather(mixed_half, "kv", axis=1, tiled=True, axis_index_groups=both_cores)
    return (mixed, landed, landed_ids.reshape(-1))


def solution(mesh):
    placed = (
        P(),
        P(("kv", "tp"), None, None, None),
        P(("kv", "tp"), None),
        P(("kv", "tp"), None, None, None),
        P(("kv", "tp")),
        P(("kv", "tp"), None),
        P("kv", "tp"),
    )
    return jax.shard_map(
        local,
        mesh=mesh,
        in_specs=placed,
        out_specs=(P(None, "tp"), P(("kv", "tp"), None, None, None), P(("kv", "tp"))),
        check_vma=False,
    )
```

```python
import math

import jax
import jax.numpy as jnp
from jax import lax
from jax.experimental import pallas as pl
from jax.experimental.pallas import tpu as pltpu
from jax.sharding import PartitionSpec as P

HQ = 64
KVH = 4
HD = 128
GROUP = 16
B = 4
PAGE = 8
CAP = 2
CHIPS = 16
NEG = -1e30
SMALL = 8 * 2**20
LARGE = 56 * 2**20

VMEM = pl.BlockSpec(memory_space=pltpu.VMEM)
ANY = pl.BlockSpec(memory_space=pl.ANY)
SMEM = pl.BlockSpec(memory_space=pltpu.SMEM)
F32 = jnp.float32
BF16 = jnp.bfloat16


def iota(shape, dim):
    return lax.broadcasted_iota(jnp.int32, shape, dim)


def round_up(x):
    return (x + jnp.abs(x) * 2.0**-7).astype(BF16).astype(F32)


def token_rows(ref, part):
    pages = ref[:, part].astype(F32)
    return pages.reshape(pages.shape[0] * PAGE, KVH * HD).astype(BF16)


def side_lanes(lane, shift, weight_sum):
    high = weight_sum.astype(BF16).astype(F32)
    return jnp.where(lane == 0, shift, jnp.where(lane == 1, high, jnp.where(lane == 4, weight_sum - high, 0.0)))


def attend_kernel(q_ref, res_ref, move_ref, count_ref, request_ref, owner_ref, request_row_ref, out_ref):
    rows = GROUP * B
    n_res, n_move = res_ref.shape[0], move_ref.shape[0]
    page = iota((8, n_res * PAGE), 1) // PAGE
    end = jnp.int32(0)
    res_request = jnp.zeros_like(page)
    for b in range(B - 1):
        end = end + count_ref[0, b]
        res_request = res_request + (page >= end).astype(jnp.int32)
    page = iota((8, n_move * PAGE), 1) // PAGE
    move_request = jnp.zeros_like(page)
    for p in range(n_move):
        move_request = jnp.where(page == p, request_ref[p], move_request)
    token_request = jnp.concatenate([res_request, move_request], axis=1)
    wanted = iota((8, token_request.shape[1]), 0) % B == token_request
    wanted = jnp.concatenate([wanted.astype(F32)] * (rows // 8), axis=0) > 0.5

    keys = jnp.concatenate([token_rows(res_ref, 0), token_rows(move_ref, 0)], axis=0)
    values = jnp.concatenate([token_rows(res_ref, 1), token_rows(move_ref, 1)], axis=0)
    q = q_ref[...].astype(F32)

    owner = owner_ref[...]
    column = jnp.sum(
        jnp.where(iota((n_move, n_move), 0) == iota((n_move, n_move), 1), owner, 0), axis=1, keepdims=True
    )
    before = (column == owner) & (iota((n_move, n_move), 0) < iota((n_move, n_move), 1))
    rank = jnp.sum(before.astype(jnp.int32), axis=0, keepdims=True)
    all_rows = out_ref.shape[0] * 8
    named = iota((all_rows, n_move), 0) // 8 == owner
    marks = request_row_ref[...] + 1
    slot_ids = [
        (jnp.sum(jnp.where(named & (rank == r), marks, 0), axis=1, keepdims=True) - 1).astype(F32)
        for r in range(CAP)
    ]

    lane = iota((rows, HD), 1)
    per = rows // 8
    for g in range(KVH):
        heads = [q[:, (g * GROUP + i) * HD : (g * GROUP + i + 1) * HD] for i in range(GROUP)]
        q_rows = jnp.concatenate(heads, axis=0).astype(BF16)
        scores = lax.dot_general(
            q_rows, keys[:, g * HD : (g + 1) * HD], (((1,), (1,)), ((), ())), preferred_element_type=F32
        ) * (1.0 / math.sqrt(HD))
        scores = jnp.where(wanted, scores, NEG)
        shift = round_up(jnp.max(scores, axis=1, keepdims=True))
        weights = jnp.where(wanted, jnp.exp(scores - shift), 0.0).astype(BF16)
        weight_sum = jnp.sum(weights.astype(F32), axis=1, keepdims=True)
        summed = jnp.dot(weights, values[:, g * HD : (g + 1) * HD], preferred_element_type=F32)
        own = slice(g * rows, (g + 1) * rows)
        extra = side_lanes(lane, shift, weight_sum)
        for r in range(CAP):
            extra = jnp.where(lane == 2 + r, slot_ids[r][own], extra)
        both = jnp.concatenate([summed.reshape(per, 8, HD), extra.reshape(per, 8, HD)], axis=1)
        out_ref[g * per : (g + 1) * per] = both.astype(BF16)


FAR = 8
QUAD = 4
HOME = QUAD * FAR
GIVEN = QUAD * (FAR - 1)


def copy_all(copies, sems):
    running = [pltpu.make_async_copy(a, b, sems.at[n]) for n, (a, b) in enumerate(copies)]
    for copy in running:
        copy.start()
    for copy in running:
        copy.wait()


def quads(ref, first, count=1):
    return ref.at[pl.ds(first * QUAD, count * QUAD)]


def pack_kernel(move_ref, owner_ref, own_out, other_out, slots_ref, used_ref, sems):
    slots_ref[...] = jnp.zeros(slots_ref.shape, slots_ref.dtype)
    for o in range(used_ref.shape[0]):
        used_ref[o] = 0
    me = lax.axis_index("kv")
    chip, core = me // 2, me % 2

    def place(p, carry):
        owner = owner_ref[p]
        rank = used_ref[owner]
        used_ref[owner] = rank + 1
        up = (owner // 2 - chip) & (CHIPS - 1)
        lands = owner % 2
        carrier = jnp.where(up == 0, lands, jnp.where(up == FAR, core, (up > FAR).astype(jnp.int32)))
        distance = jnp.where(up > FAR, CHIPS - up, up)
        slot = (distance - 1) * 4 + jnp.where(lands == carrier, 0, CAP)
        slot = jnp.where(up == 0, jnp.where(carrier == core, HOME, GIVEN), slot)
        slots_ref[jnp.where(carrier == core, slot, HOME + CAP + slot) + rank] = move_ref[p]
        return carry

    lax.fori_loop(0, move_ref.shape[0], place, 0, unroll=8)
    own, other = slots_ref.at[pl.ds(0, HOME + CAP)], slots_ref.at[pl.ds(HOME + CAP, GIVEN + CAP)]
    copy_all([(other, other_out), (own, own_out)], sems)


def short_kernel(own_ref, got_ref, after_ref, one_ref, two_ref, sems):
    del after_ref
    copies = []
    for n, ref in enumerate((one_ref, two_ref)):
        for m in range(3):
            copies.append((quads(own_ref, n + 3 * m), quads(ref, 2 * m)))
            if n + 3 * m < FAR - 1:
                copies.append((quads(got_ref, n + 3 * m), quads(ref, 2 * m + 1)))
    copy_all(copies, sems)


def long_copies(first, own_ref, got_ref, one_ref, two_ref, out_ref):
    n = first // 3 - 1
    count = 2 - n
    return [
        (quads(own_ref, first - 1), quads(out_ref, 0)),
        (quads(got_ref, first - 1), quads(out_ref, 1)),
        (quads(one_ref, 2 + 2 * n, 2), quads(out_ref, 2, 2)),
        (quads(two_ref, 2 + 2 * n, count), quads(out_ref, 4, count)),
    ]


def three_kernel(own_ref, got_ref, one_ref, two_ref, out_ref, sems):
    copy_all(long_copies(3, own_ref, got_ref, one_ref, two_ref, out_ref), sems)


def six_kernel(own_ref, got_ref, one_ref, two_ref, after_ref, out_ref, sems):
    del after_ref
    copy_all(long_copies(6, own_ref, got_ref, one_ref, two_ref, out_ref), sems)


def arrived(one_ref, two_ref, three_ref, six_ref):
    return (
        (1, one_ref, 0),
        (2, two_ref, 0),
        (3, three_ref, 0),
        (4, three_ref, 2),
        (5, three_ref, 4),
        (6, six_ref, 0),
        (7, six_ref, 2),
    )


def give_kernel(one_ref, two_ref, three_ref, six_ref, after_ref, out_ref, sems):
    del after_ref
    core = lax.axis_index("kv") % 2
    copies = [(six_ref.at[pl.ds(4 * QUAD + CAP, CAP)], out_ref.at[pl.ds(GIVEN, CAP)])]
    for distance, ref, quad in arrived(one_ref, two_ref, three_ref, six_ref):
        for quad, start in ((quad, core), (quad + 1, 1 - core)):
            to = out_ref.at[pl.ds((distance - 1) * QUAD + start * CAP, CAP)]
            copies.append((ref.at[pl.ds(quad * QUAD + CAP, CAP)], to))
    copy_all(copies, sems)


def rows(out_ref, up, start=0, count=CAP):
    chip = lax.axis_index("kv") // 2
    return out_ref.at[pl.ds(((chip + up) & (CHIPS - 1)) * QUAD + start * CAP, count)]


def land_kernel(own_ref, got_ref, one_ref, two_ref, three_ref, six_ref, out_ref, sems):
    core = lax.axis_index("kv") % 2
    way = 1 - 2 * core
    copies = [
        (own_ref.at[pl.ds(HOME, CAP)], rows(out_ref, 0, core)),
        (got_ref.at[pl.ds(GIVEN, CAP)], rows(out_ref, 0, 1 - core)),
        (six_ref.at[pl.ds(4 * QUAD, CAP)], rows(out_ref, FAR, core)),
    ]
    for distance, ref, quad in arrived(one_ref, two_ref, three_ref, six_ref):
        for quad, start in ((quad, core), (quad + 1, 1 - core)):
            copies.append((ref.at[pl.ds(quad * QUAD, CAP)], rows(out_ref, -way * distance, start)))
    copy_all(copies, sems)


def land_taken_kernel(taken_any, landed_ref, after_ref, out_ref, taken_ref, sems):
    del landed_ref, after_ref
    core = lax.axis_index("kv") % 2
    way = 1 - 2 * core
    pltpu.sync_copy(taken_any, taken_ref)
    copies = [(taken_ref.at[pl.ds(GIVEN, CAP)], rows(out_ref, FAR, 1 - core))]
    for distance in range(1, FAR):
        copies.append((quads(taken_ref, distance - 1), rows(out_ref, way * distance, 0, QUAD)))
    copy_all(copies, sems)


def combined(parts):
    shifts, values = parts[:, 8:, 0:1], parts[:, :8, :]
    sums = parts[:, 8:, 1:2] + parts[:, 8:, 4:5]
    shift = jnp.max(shifts, axis=0)
    factor = jnp.exp(shifts - shift[None])
    return shift, jnp.sum(sums * factor, axis=0), jnp.sum(values * factor, axis=0)


def fill_kernel(*refs):
    del refs


def column_kernel(parts_any, after_ref, out_ref, ids_ref, parts_ref):
    del after_ref
    pltpu.sync_copy(parts_any, parts_ref)
    parts = parts_ref[...].astype(F32)
    shift, weight_sum, values = combined(parts)
    lane = iota((8, HD), 1)
    extra = side_lanes(lane, shift, weight_sum)
    out = jnp.concatenate([values, extra], axis=0).astype(out_ref.dtype)
    out_ref[...] = jnp.broadcast_to(out[None], out_ref.shape)
    n = parts.shape[0]
    source, place = iota((n, n * CAP), 0), iota((n, n * CAP), 1)
    ids = parts[:, 8, :]
    ids = jnp.where(place % CAP == 0, ids[:, 2:3], ids[:, 3:4])
    ids_ref[...] = jnp.sum(jnp.where(source == place // CAP, ids, 0.0), axis=0, keepdims=True).astype(jnp.int32)


def project_kernel(parts_any, weight_ref, out_ref, parts_ref):
    pltpu.sync_copy(parts_any, parts_ref)
    _, weight_sum, values = combined(parts_ref[...].astype(F32))
    attended = (values / weight_sum).astype(BF16)
    upper = jnp.dot(attended, weight_ref[:HD], preferred_element_type=F32)
    lower = jnp.dot(attended, weight_ref[HD:], preferred_element_type=F32)
    out_ref[...] = upper[:B] + lower[B:]


def pair_kernel(parts_any, out_ref, parts_ref):
    pltpu.sync_copy(parts_any, parts_ref)
    both = (parts_ref[0] + parts_ref[1]).astype(out_ref.dtype)
    out_ref[...] = jnp.broadcast_to(both[None], out_ref.shape)


def add_kernel(parts_any, own_ref, out_ref, passed_ref, parts_ref):
    del own_ref, passed_ref
    pltpu.sync_copy(parts_any, parts_ref)
    out_ref[...] = jnp.sum(parts_ref[...].astype(F32), axis=0).astype(out_ref.dtype)


def local(queries, res_cache, res_count, move_cache, move_request, move_owner, out_weight):
    kv_size, tp_size = lax.axis_size("kv"), lax.axis_size("tp")
    owners = move_owner.reshape(-1)
    page = move_cache.shape[1:]

    def pages(n):
        return jax.ShapeDtypeStruct((n,) + page, BF16)

    def shift(x, chips):
        pairs = [(i, (i + 2 * chips * (1 - 2 * (i % 2))) % kv_size) for i in range(kv_size)]
        return lax.ppermute(x, "kv", pairs)

    def swap(x):
        return lax.ppermute(x, "kv", [(i, i ^ 1) for i in range(kv_size)])

    own, other = pl.pallas_call(
        pack_kernel,
        out_shape=(pages(HOME + CAP), pages(GIVEN + CAP)),
        in_specs=[VMEM, SMEM],
        out_specs=(ANY, ANY),
        scratch_shapes=[
            pltpu.VMEM((HOME + GIVEN + 2 * CAP,) + page, BF16),
            pltpu.SMEM((kv_size,), jnp.int32),
            pltpu.SemaphoreType.DMA((2,)),
        ],
        compiler_params=pltpu.CompilerParams(vmem_limit_bytes=LARGE),
        name="pack",
    )(move_cache, owners)
    got = swap(other)
    def copies(kernel, name, out_pages, count, *args):
        return pl.pallas_call(
            kernel,
            out_shape=tuple(pages(n) for n in out_pages),
            in_specs=[ANY] * len(args),
            out_specs=(ANY,) * len(out_pages),
            scratch_shapes=[pltpu.SemaphoreType.DMA((count,))],
            compiler_params=pltpu.CompilerParams(vmem_limit_bytes=SMALL),
            cost_estimate=pl.CostEstimate(flops=0, bytes_accessed=1024, transcendentals=0),
            name=name,
        )(*args)

    parts = pl.pallas_call(
        attend_kernel,
        out_shape=jax.ShapeDtypeStruct((kv_size, 16, HD), BF16),
        in_specs=[VMEM, VMEM, VMEM, SMEM, SMEM, VMEM, VMEM],
        out_specs=VMEM,
        name="attend",
    )(queries, res_cache, move_cache, res_count, move_request, owners[None, :], move_request[None, :])
    one, two = copies(short_kernel, "short", (6 * QUAD, 5 * QUAD), 11, own, got, parts)
    one, two = shift(one, 1), shift(two, 2)
    parts = lax.all_to_all(parts, "kv", split_axis=0, concat_axis=0, tiled=True)
    (three,) = copies(three_kernel, "three", (6 * QUAD,), 4, own, got, one, two)
    (six,) = copies(six_kernel, "six", (5 * QUAD,), 4, own, got, one, two, three)
    six_up, three_up = shift(six, 6), shift(three, 3)
    own = pl.pallas_call(
        fill_kernel,
        out_shape=pages(HOME + CAP),
        in_specs=[ANY],
        out_specs=ANY,
        input_output_aliases={0: 0},
        compiler_params=pltpu.CompilerParams(vmem_limit_bytes=SMALL),
        cost_estimate=pl.CostEstimate(flops=10**11, bytes_accessed=1024, transcendentals=0),
        name="fill",
    )(own)
    part, landed_ids = pl.pallas_call(
        column_kernel,
        out_shape=(
            jax.ShapeDtypeStruct((tp_size, 16, HD), BF16),
            jax.ShapeDtypeStruct((1, kv_size * CAP), jnp.int32),
        ),
        in_specs=[ANY, ANY],
        out_specs=(VMEM, VMEM),
        scratch_shapes=[pltpu.VMEM(parts.shape, BF16)],
        compiler_params=pltpu.CompilerParams(vmem_limit_bytes=SMALL),
        name="column",
        cost_estimate=pl.CostEstimate(flops=0, bytes_accessed=1024, transcendentals=0),
    )(parts, own)
    six, three = six_up, three_up
    columns = lax.all_to_all(part, "tp", split_axis=0, concat_axis=0, tiled=True)
    partial_out = pl.pallas_call(
        project_kernel,
        out_shape=jax.ShapeDtypeStruct((B, out_weight.shape[1]), F32),
        in_specs=[ANY, VMEM],
        out_specs=VMEM,
        scratch_shapes=[pltpu.VMEM(columns.shape, BF16)],
        compiler_params=pltpu.CompilerParams(vmem_limit_bytes=SMALL),
        name="project",
    )(columns, out_weight)
    pair = lax.all_gather(
        partial_out, "kv", axis_index_groups=[[2 * z, 2 * z + 1] for z in range(CHIPS)]
    )
    chip_out = pl.pallas_call(
        pair_kernel,
        out_shape=jax.ShapeDtypeStruct((CHIPS, B, out_weight.shape[1]), BF16),
        in_specs=[ANY],
        out_specs=VMEM,
        scratch_shapes=[pltpu.VMEM(pair.shape, F32)],
        compiler_params=pltpu.CompilerParams(vmem_limit_bytes=SMALL),
        name="pair",
    )(pair)
    partials = lax.all_to_all(
        chip_out,
        "kv",
        split_axis=0,
        concat_axis=0,
        tiled=True,
        axis_index_groups=[[2 * z + c for z in range(CHIPS)] for c in range(2)],
    )
    (give,) = copies(give_kernel, "give", (GIVEN + CAP,), 15, one, two, three, six, chip_out)
    taken = swap(give)
    (landed,) = copies(land_kernel, "land", (kv_size * CAP,), 17, own, got, one, two, three, six)
    mixed, own = pl.pallas_call(
        add_kernel,
        out_shape=(jax.ShapeDtypeStruct((B, out_weight.shape[1]), BF16), pages(HOME + CAP)),
        in_specs=[ANY, ANY],
        out_specs=(VMEM, ANY),
        input_output_aliases={1: 1},
        scratch_shapes=[pltpu.VMEM(partials.shape, BF16)],
        compiler_params=pltpu.CompilerParams(vmem_limit_bytes=SMALL),
        name="add",
    )(partials, own)
    landed = pl.pallas_call(
        land_taken_kernel,
        out_shape=pages(kv_size * CAP),
        in_specs=[ANY] * 3,
        out_specs=ANY,
        input_output_aliases={1: 0},
        scratch_shapes=[pltpu.VMEM(taken.shape, BF16), pltpu.SemaphoreType.DMA((FAR,))],
        compiler_params=pltpu.CompilerParams(vmem_limit_bytes=SMALL),
        cost_estimate=pl.CostEstimate(flops=0, bytes_accessed=1024, transcendentals=0),
        name="land_taken",
    )(taken, landed, own)
    return (mixed, landed, landed_ids.reshape(-1))


def solution(mesh):
    placed = (
        P(),
        P(("kv", "tp"), None, None, None),
        P(("kv", "tp"), None),
        P(("kv", "tp"), None, None, None),
        P(("kv", "tp")),
        P(("kv", "tp"), None),
        P("kv", "tp"),
    )
    return jax.shard_map(
        local,
        mesh=mesh,
        in_specs=placed,
        out_specs=(P(None, "tp"), P(("kv", "tp"), None, None, None), P(("kv", "tp"))),
        check_vma=False,
    )
```

```python
import math

import jax
import jax.numpy as jnp
from jax import lax
from jax.experimental import pallas as pl
from jax.experimental.pallas import tpu as pltpu
from jax.sharding import PartitionSpec as P

HQ = 64
KVH = 4
HD = 128
GROUP = 16
B = 4
PAGE = 8
CAP = 2
CHIPS = 16
NEG = -1e30
SMALL = 8 * 2**20
LARGE = 56 * 2**20

VMEM = pl.BlockSpec(memory_space=pltpu.VMEM)
ANY = pl.BlockSpec(memory_space=pl.ANY)
SMEM = pl.BlockSpec(memory_space=pltpu.SMEM)
F32 = jnp.float32
BF16 = jnp.bfloat16


def iota(shape, dim):
    return lax.broadcasted_iota(jnp.int32, shape, dim)


def round_up(x):
    return (x + jnp.abs(x) * 2.0**-7).astype(BF16).astype(F32)


def token_rows(ref, part):
    pages = ref[:, part].astype(F32)
    return pages.reshape(pages.shape[0] * PAGE, KVH * HD).astype(BF16)


def side_lanes(lane, shift, weight_sum):
    high = weight_sum.astype(BF16).astype(F32)
    return jnp.where(lane == 0, shift, jnp.where(lane == 1, high, jnp.where(lane == 4, weight_sum - high, 0.0)))


def attend_kernel(q_ref, res_ref, move_ref, count_ref, request_ref, owner_ref, request_row_ref, out_ref):
    rows = GROUP * B
    n_res, n_move = res_ref.shape[0], move_ref.shape[0]
    page = iota((8, n_res * PAGE), 1) // PAGE
    end = jnp.int32(0)
    res_request = jnp.zeros_like(page)
    for b in range(B - 1):
        end = end + count_ref[0, b]
        res_request = res_request + (page >= end).astype(jnp.int32)
    page = iota((8, n_move * PAGE), 1) // PAGE
    move_request = jnp.zeros_like(page)
    for p in range(n_move):
        move_request = jnp.where(page == p, request_ref[p], move_request)
    token_request = jnp.concatenate([res_request, move_request], axis=1)
    wanted = iota((8, token_request.shape[1]), 0) % B == token_request
    wanted = jnp.concatenate([wanted.astype(F32)] * (rows // 8), axis=0) > 0.5

    keys = jnp.concatenate([token_rows(res_ref, 0), token_rows(move_ref, 0)], axis=0)
    values = jnp.concatenate([token_rows(res_ref, 1), token_rows(move_ref, 1)], axis=0)
    q = q_ref[...].astype(F32)

    owner = owner_ref[...]
    column = jnp.sum(
        jnp.where(iota((n_move, n_move), 0) == iota((n_move, n_move), 1), owner, 0), axis=1, keepdims=True
    )
    before = (column == owner) & (iota((n_move, n_move), 0) < iota((n_move, n_move), 1))
    rank = jnp.sum(before.astype(jnp.int32), axis=0, keepdims=True)
    all_rows = out_ref.shape[0] * 8
    named = iota((all_rows, n_move), 0) // 8 == owner
    marks = request_row_ref[...] + 1
    slot_ids = [
        (jnp.sum(jnp.where(named & (rank == r), marks, 0), axis=1, keepdims=True) - 1).astype(F32)
        for r in range(CAP)
    ]

    lane = iota((rows, HD), 1)
    per = rows // 8
    for g in range(KVH):
        heads = [q[:, (g * GROUP + i) * HD : (g * GROUP + i + 1) * HD] for i in range(GROUP)]
        q_rows = jnp.concatenate(heads, axis=0).astype(BF16)
        scores = lax.dot_general(
            q_rows, keys[:, g * HD : (g + 1) * HD], (((1,), (1,)), ((), ())), preferred_element_type=F32
        ) * (1.0 / math.sqrt(HD))
        scores = jnp.where(wanted, scores, NEG)
        shift = round_up(jnp.max(scores, axis=1, keepdims=True))
        weights = jnp.where(wanted, jnp.exp(scores - shift), 0.0).astype(BF16)
        weight_sum = jnp.sum(weights.astype(F32), axis=1, keepdims=True)
        summed = jnp.dot(weights, values[:, g * HD : (g + 1) * HD], preferred_element_type=F32)
        own = slice(g * rows, (g + 1) * rows)
        extra = side_lanes(lane, shift, weight_sum)
        for r in range(CAP):
            extra = jnp.where(lane == 2 + r, slot_ids[r][own], extra)
        both = jnp.concatenate([summed.reshape(per, 8, HD), extra.reshape(per, 8, HD)], axis=1)
        out_ref[g * per : (g + 1) * per] = both.astype(BF16)


FAR = 8
QUAD = 4
HOME = QUAD * FAR
GIVEN = QUAD * (FAR - 1)


def copy_all(copies, sems):
    running = [pltpu.make_async_copy(a, b, sems.at[n]) for n, (a, b) in enumerate(copies)]
    for copy in running:
        copy.start()
    for copy in running:
        copy.wait()


def quads(ref, first, count=1):
    return ref.at[pl.ds(first * QUAD, count * QUAD)]


def pack_kernel(move_ref, owner_ref, own_out, other_out, slots_ref, used_ref, sems):
    slots_ref[...] = jnp.zeros(slots_ref.shape, slots_ref.dtype)
    for o in range(used_ref.shape[0]):
        used_ref[o] = 0
    me = lax.axis_index("kv")
    chip, core = me // 2, me % 2

    def place(p, carry):
        owner = owner_ref[p]
        rank = used_ref[owner]
        used_ref[owner] = rank + 1
        up = (owner // 2 - chip) & (CHIPS - 1)
        lands = owner % 2
        carrier = jnp.where(up == 0, lands, jnp.where(up == FAR, core, (up > FAR).astype(jnp.int32)))
        distance = jnp.where(up > FAR, CHIPS - up, up)
        slot = (distance - 1) * 4 + jnp.where(lands == carrier, 0, CAP)
        slot = jnp.where(up == 0, jnp.where(carrier == core, HOME, GIVEN), slot)
        slots_ref[jnp.where(carrier == core, slot, HOME + CAP + slot) + rank] = move_ref[p]
        return carry

    lax.fori_loop(0, move_ref.shape[0], place, 0, unroll=8)
    own, other = slots_ref.at[pl.ds(0, HOME + CAP)], slots_ref.at[pl.ds(HOME + CAP, GIVEN + CAP)]
    copy_all([(other, other_out), (own, own_out)], sems)


def short_copies(n, own_ref, got_ref, out_ref):
    copies = []
    for m in range(3):
        copies.append((quads(own_ref, n + 3 * m), quads(out_ref, 2 * m)))
        if n + 3 * m < FAR - 1:
            copies.append((quads(got_ref, n + 3 * m), quads(out_ref, 2 * m + 1)))
    return copies


def one_kernel(own_ref, got_ref, after_ref, out_ref, sems):
    del after_ref
    copy_all(short_copies(0, own_ref, got_ref, out_ref), sems)


def two_kernel(own_ref, got_ref, after_ref, out_ref, sems):
    del after_ref
    copy_all(short_copies(1, own_ref, got_ref, out_ref), sems)


def long_copies(first, own_ref, got_ref, one_ref, two_ref, out_ref):
    n = first // 3 - 1
    count = 2 - n
    return [
        (quads(own_ref, first - 1), quads(out_ref, 0)),
        (quads(got_ref, first - 1), quads(out_ref, 1)),
        (quads(one_ref, 2 + 2 * n, 2), quads(out_ref, 2, 2)),
        (quads(two_ref, 2 + 2 * n, count), quads(out_ref, 4, count)),
    ]


def three_kernel(own_ref, got_ref, one_ref, two_ref, out_ref, sems):
    copy_all(long_copies(3, own_ref, got_ref, one_ref, two_ref, out_ref), sems)


def six_kernel(own_ref, got_ref, one_ref, two_ref, after_ref, out_ref, sems):
    del after_ref
    copy_all(long_copies(6, own_ref, got_ref, one_ref, two_ref, out_ref), sems)


def arrived(one_ref, two_ref, three_ref, six_ref):
    return (
        (1, one_ref, 0),
        (2, two_ref, 0),
        (3, three_ref, 0),
        (4, three_ref, 2),
        (5, three_ref, 4),
        (6, six_ref, 0),
        (7, six_ref, 2),
    )


def give_kernel(one_ref, two_ref, three_ref, six_ref, after_ref, out_ref, sems):
    del after_ref
    core = lax.axis_index("kv") % 2
    copies = [(six_ref.at[pl.ds(4 * QUAD + CAP, CAP)], out_ref.at[pl.ds(GIVEN, CAP)])]
    for distance, ref, quad in arrived(one_ref, two_ref, three_ref, six_ref):
        for quad, start in ((quad, core), (quad + 1, 1 - core)):
            to = out_ref.at[pl.ds((distance - 1) * QUAD + start * CAP, CAP)]
            copies.append((ref.at[pl.ds(quad * QUAD + CAP, CAP)], to))
    copy_all(copies, sems)


def rows(out_ref, up, start=0, count=CAP):
    chip = lax.axis_index("kv") // 2
    return out_ref.at[pl.ds(((chip + up) & (CHIPS - 1)) * QUAD + start * CAP, count)]


def land_kernel(own_ref, got_ref, one_ref, two_ref, three_ref, six_ref, out_ref, sems):
    core = lax.axis_index("kv") % 2
    way = 1 - 2 * core
    copies = [
        (own_ref.at[pl.ds(HOME, CAP)], rows(out_ref, 0, core)),
        (got_ref.at[pl.ds(GIVEN, CAP)], rows(out_ref, 0, 1 - core)),
        (six_ref.at[pl.ds(4 * QUAD, CAP)], rows(out_ref, FAR, core)),
    ]
    for distance, ref, quad in arrived(one_ref, two_ref, three_ref, six_ref):
        for quad, start in ((quad, core), (quad + 1, 1 - core)):
            copies.append((ref.at[pl.ds(quad * QUAD, CAP)], rows(out_ref, -way * distance, start)))
    copy_all(copies, sems)


def land_taken_kernel(taken_any, landed_ref, after_ref, out_ref, taken_ref, sems):
    del landed_ref, after_ref
    core = lax.axis_index("kv") % 2
    way = 1 - 2 * core
    pltpu.sync_copy(taken_any, taken_ref)
    copies = [(taken_ref.at[pl.ds(GIVEN, CAP)], rows(out_ref, FAR, 1 - core))]
    for distance in range(1, FAR):
        copies.append((quads(taken_ref, distance - 1), rows(out_ref, way * distance, 0, QUAD)))
    copy_all(copies, sems)


def combined(parts):
    shifts, values = parts[:, 8:, 0:1], parts[:, :8, :]
    sums = parts[:, 8:, 1:2] + parts[:, 8:, 4:5]
    shift = jnp.max(shifts, axis=0)
    factor = jnp.exp(shifts - shift[None])
    return shift, jnp.sum(sums * factor, axis=0), jnp.sum(values * factor, axis=0)


def fill_kernel(*refs):
    del refs


def column_kernel(parts_any, after_ref, out_ref, ids_ref, parts_ref):
    del after_ref
    pltpu.sync_copy(parts_any, parts_ref)
    parts = parts_ref[...].astype(F32)
    shift, weight_sum, values = combined(parts)
    lane = iota((8, HD), 1)
    extra = side_lanes(lane, shift, weight_sum)
    out = jnp.concatenate([values, extra], axis=0).astype(out_ref.dtype)
    out_ref[...] = jnp.broadcast_to(out[None], out_ref.shape)
    n = parts.shape[0]
    source, place = iota((n, n * CAP), 0), iota((n, n * CAP), 1)
    ids = parts[:, 8, :]
    ids = jnp.where(place % CAP == 0, ids[:, 2:3], ids[:, 3:4])
    ids_ref[...] = jnp.sum(jnp.where(source == place // CAP, ids, 0.0), axis=0, keepdims=True).astype(jnp.int32)


def project_kernel(parts_any, weight_ref, out_ref, parts_ref):
    pltpu.sync_copy(parts_any, parts_ref)
    _, weight_sum, values = combined(parts_ref[...].astype(F32))
    attended = (values / weight_sum).astype(BF16)
    upper = jnp.dot(attended, weight_ref[:HD], preferred_element_type=F32)
    lower = jnp.dot(attended, weight_ref[HD:], preferred_element_type=F32)
    out_ref[...] = upper[:B] + lower[B:]


def pair_kernel(parts_any, out_ref, parts_ref):
    pltpu.sync_copy(parts_any, parts_ref)
    both = (parts_ref[0] + parts_ref[1]).astype(out_ref.dtype)
    out_ref[...] = jnp.broadcast_to(both[None], out_ref.shape)


def add_kernel(parts_any, own_ref, out_ref, passed_ref, parts_ref):
    del own_ref, passed_ref
    pltpu.sync_copy(parts_any, parts_ref)
    out_ref[...] = jnp.sum(parts_ref[...].astype(F32), axis=0).astype(out_ref.dtype)


def local(queries, res_cache, res_count, move_cache, move_request, move_owner, out_weight):
    kv_size, tp_size = lax.axis_size("kv"), lax.axis_size("tp")
    owners = move_owner.reshape(-1)
    page = move_cache.shape[1:]

    def pages(n):
        return jax.ShapeDtypeStruct((n,) + page, BF16)

    def shift(x, chips):
        pairs = [(i, (i + 2 * chips * (1 - 2 * (i % 2))) % kv_size) for i in range(kv_size)]
        return lax.ppermute(x, "kv", pairs)

    def swap(x):
        return lax.ppermute(x, "kv", [(i, i ^ 1) for i in range(kv_size)])

    own, other = pl.pallas_call(
        pack_kernel,
        out_shape=(pages(HOME + CAP), pages(GIVEN + CAP)),
        in_specs=[VMEM, SMEM],
        out_specs=(ANY, ANY),
        scratch_shapes=[
            pltpu.VMEM((HOME + GIVEN + 2 * CAP,) + page, BF16),
            pltpu.SMEM((kv_size,), jnp.int32),
            pltpu.SemaphoreType.DMA((2,)),
        ],
        compiler_params=pltpu.CompilerParams(vmem_limit_bytes=LARGE),
        name="pack",
    )(move_cache, owners)
    got = swap(other)
    def copies(kernel, name, out_pages, count, *args):
        return pl.pallas_call(
            kernel,
            out_shape=tuple(pages(n) for n in out_pages),
            in_specs=[ANY] * len(args),
            out_specs=(ANY,) * len(out_pages),
            scratch_shapes=[pltpu.SemaphoreType.DMA((count,))],
            compiler_params=pltpu.CompilerParams(vmem_limit_bytes=SMALL),
            cost_estimate=pl.CostEstimate(flops=0, bytes_accessed=1024, transcendentals=0),
            name=name,
        )(*args)

    parts = pl.pallas_call(
        attend_kernel,
        out_shape=jax.ShapeDtypeStruct((kv_size, 16, HD), BF16),
        in_specs=[VMEM, VMEM, VMEM, SMEM, SMEM, VMEM, VMEM],
        out_specs=VMEM,
        name="attend",
    )(queries, res_cache, move_cache, res_count, move_request, owners[None, :], move_request[None, :])
    (one,) = copies(one_kernel, "one", (6 * QUAD,), 6, own, got, parts)
    (two,) = copies(two_kernel, "two", (5 * QUAD,), 5, own, got, one)
    one, two = shift(one, 1), shift(two, 2)
    parts = lax.all_to_all(parts, "kv", split_axis=0, concat_axis=0, tiled=True)
    (three,) = copies(three_kernel, "three", (6 * QUAD,), 4, own, got, one, two)
    (six,) = copies(six_kernel, "six", (5 * QUAD,), 4, own, got, one, two, three)
    six_up, three_up = shift(six, 6), shift(three, 3)
    own = pl.pallas_call(
        fill_kernel,
        out_shape=pages(HOME + CAP),
        in_specs=[ANY],
        out_specs=ANY,
        input_output_aliases={0: 0},
        compiler_params=pltpu.CompilerParams(vmem_limit_bytes=SMALL),
        cost_estimate=pl.CostEstimate(flops=10**11, bytes_accessed=1024, transcendentals=0),
        name="fill",
    )(own)
    part, landed_ids = pl.pallas_call(
        column_kernel,
        out_shape=(
            jax.ShapeDtypeStruct((tp_size, 16, HD), BF16),
            jax.ShapeDtypeStruct((1, kv_size * CAP), jnp.int32),
        ),
        in_specs=[ANY, ANY],
        out_specs=(VMEM, VMEM),
        scratch_shapes=[pltpu.VMEM(parts.shape, BF16)],
        compiler_params=pltpu.CompilerParams(vmem_limit_bytes=SMALL),
        name="column",
        cost_estimate=pl.CostEstimate(flops=0, bytes_accessed=1024, transcendentals=0),
    )(parts, own)
    six, three = six_up, three_up
    columns = lax.all_to_all(part, "tp", split_axis=0, concat_axis=0, tiled=True)
    partial_out = pl.pallas_call(
        project_kernel,
        out_shape=jax.ShapeDtypeStruct((B, out_weight.shape[1]), F32),
        in_specs=[ANY, VMEM],
        out_specs=VMEM,
        scratch_shapes=[pltpu.VMEM(columns.shape, BF16)],
        compiler_params=pltpu.CompilerParams(vmem_limit_bytes=SMALL),
        name="project",
    )(columns, out_weight)
    pair = lax.all_gather(
        partial_out, "kv", axis_index_groups=[[2 * z, 2 * z + 1] for z in range(CHIPS)]
    )
    chip_out = pl.pallas_call(
        pair_kernel,
        out_shape=jax.ShapeDtypeStruct((CHIPS, B, out_weight.shape[1]), BF16),
        in_specs=[ANY],
        out_specs=VMEM,
        scratch_shapes=[pltpu.VMEM(pair.shape, F32)],
        compiler_params=pltpu.CompilerParams(vmem_limit_bytes=SMALL),
        name="pair",
    )(pair)
    partials = lax.all_to_all(
        chip_out,
        "kv",
        split_axis=0,
        concat_axis=0,
        tiled=True,
        axis_index_groups=[[2 * z + c for z in range(CHIPS)] for c in range(2)],
    )
    (give,) = copies(give_kernel, "give", (GIVEN + CAP,), 15, one, two, three, six, chip_out)
    taken = swap(give)
    (landed,) = copies(land_kernel, "land", (kv_size * CAP,), 17, own, got, one, two, three, six)
    mixed, own = pl.pallas_call(
        add_kernel,
        out_shape=(jax.ShapeDtypeStruct((B, out_weight.shape[1]), BF16), pages(HOME + CAP)),
        in_specs=[ANY, ANY],
        out_specs=(VMEM, ANY),
        input_output_aliases={1: 1},
        scratch_shapes=[pltpu.VMEM(partials.shape, BF16)],
        compiler_params=pltpu.CompilerParams(vmem_limit_bytes=SMALL),
        name="add",
    )(partials, own)
    landed = pl.pallas_call(
        land_taken_kernel,
        out_shape=pages(kv_size * CAP),
        in_specs=[ANY] * 3,
        out_specs=ANY,
        input_output_aliases={1: 0},
        scratch_shapes=[pltpu.VMEM(taken.shape, BF16), pltpu.SemaphoreType.DMA((FAR,))],
        compiler_params=pltpu.CompilerParams(vmem_limit_bytes=SMALL),
        cost_estimate=pl.CostEstimate(flops=0, bytes_accessed=1024, transcendentals=0),
        name="land_taken",
    )(taken, landed, own)
    return (mixed, landed, landed_ids.reshape(-1))


def solution(mesh):
    placed = (
        P(),
        P(("kv", "tp"), None, None, None),
        P(("kv", "tp"), None),
        P(("kv", "tp"), None, None, None),
        P(("kv", "tp")),
        P(("kv", "tp"), None),
        P("kv", "tp"),
    )
    return jax.shard_map(
        local,
        mesh=mesh,
        in_specs=placed,
        out_specs=(P(None, "tp"), P(("kv", "tp"), None, None, None), P(("kv", "tp"))),
        check_vma=False,
    )
```

```python
import math

import jax
import jax.numpy as jnp
from jax import lax
from jax.experimental import pallas as pl
from jax.experimental.pallas import tpu as pltpu
from jax.sharding import PartitionSpec as P

HQ = 64
KVH = 4
HD = 128
GROUP = 16
B = 4
PAGE = 8
CAP = 2
CHIPS = 16
NEG = -1e30
SMALL = 8 * 2**20
LARGE = 56 * 2**20

VMEM = pl.BlockSpec(memory_space=pltpu.VMEM)
ANY = pl.BlockSpec(memory_space=pl.ANY)
SMEM = pl.BlockSpec(memory_space=pltpu.SMEM)
F32 = jnp.float32
BF16 = jnp.bfloat16


def iota(shape, dim):
    return lax.broadcasted_iota(jnp.int32, shape, dim)


def round_up(x):
    return (x + jnp.abs(x) * 2.0**-7).astype(BF16).astype(F32)


def token_rows(ref, part):
    pages = ref[:, part].astype(F32)
    return pages.reshape(pages.shape[0] * PAGE, KVH * HD).astype(BF16)


def side_lanes(lane, shift, weight_sum):
    high = weight_sum.astype(BF16).astype(F32)
    return jnp.where(lane == 0, shift, jnp.where(lane == 1, high, jnp.where(lane == 4, weight_sum - high, 0.0)))


def attend_kernel(q_ref, res_ref, move_ref, count_ref, request_ref, owner_ref, request_row_ref, out_ref):
    rows = GROUP * B
    n_res, n_move = res_ref.shape[0], move_ref.shape[0]
    page = iota((8, n_res * PAGE), 1) // PAGE
    end = jnp.int32(0)
    res_request = jnp.zeros_like(page)
    for b in range(B - 1):
        end = end + count_ref[0, b]
        res_request = res_request + (page >= end).astype(jnp.int32)
    page = iota((8, n_move * PAGE), 1) // PAGE
    move_request = jnp.zeros_like(page)
    for p in range(n_move):
        move_request = jnp.where(page == p, request_ref[p], move_request)
    token_request = jnp.concatenate([res_request, move_request], axis=1)
    wanted = iota((8, token_request.shape[1]), 0) % B == token_request
    wanted = jnp.concatenate([wanted.astype(F32)] * (rows // 8), axis=0) > 0.5

    keys = jnp.concatenate([token_rows(res_ref, 0), token_rows(move_ref, 0)], axis=0)
    values = jnp.concatenate([token_rows(res_ref, 1), token_rows(move_ref, 1)], axis=0)
    q = q_ref[...].astype(F32)

    owner = owner_ref[...]
    column = jnp.sum(
        jnp.where(iota((n_move, n_move), 0) == iota((n_move, n_move), 1), owner, 0), axis=1, keepdims=True
    )
    before = (column == owner) & (iota((n_move, n_move), 0) < iota((n_move, n_move), 1))
    rank = jnp.sum(before.astype(jnp.int32), axis=0, keepdims=True)
    all_rows = out_ref.shape[0] * 8
    named = iota((all_rows, n_move), 0) // 8 == owner
    marks = request_row_ref[...] + 1
    slot_ids = [
        (jnp.sum(jnp.where(named & (rank == r), marks, 0), axis=1, keepdims=True) - 1).astype(F32)
        for r in range(CAP)
    ]

    lane = iota((rows, HD), 1)
    per = rows // 8
    for g in range(KVH):
        heads = [q[:, (g * GROUP + i) * HD : (g * GROUP + i + 1) * HD] for i in range(GROUP)]
        q_rows = jnp.concatenate(heads, axis=0).astype(BF16)
        scores = lax.dot_general(
            q_rows, keys[:, g * HD : (g + 1) * HD], (((1,), (1,)), ((), ())), preferred_element_type=F32
        ) * (1.0 / math.sqrt(HD))
        scores = jnp.where(wanted, scores, NEG)
        shift = round_up(jnp.max(scores, axis=1, keepdims=True))
        weights = jnp.where(wanted, jnp.exp(scores - shift), 0.0).astype(BF16)
        weight_sum = jnp.sum(weights.astype(F32), axis=1, keepdims=True)
        summed = jnp.dot(weights, values[:, g * HD : (g + 1) * HD], preferred_element_type=F32)
        own = slice(g * rows, (g + 1) * rows)
        extra = side_lanes(lane, shift, weight_sum)
        for r in range(CAP):
            extra = jnp.where(lane == 2 + r, slot_ids[r][own], extra)
        both = jnp.concatenate([summed.reshape(per, 8, HD), extra.reshape(per, 8, HD)], axis=1)
        out_ref[g * per : (g + 1) * per] = both.astype(BF16)


FAR = 8
QUAD = 4
HOME = QUAD * FAR
GIVEN = QUAD * (FAR - 1)


def copy_all(copies, sems):
    running = [pltpu.make_async_copy(a, b, sems.at[n]) for n, (a, b) in enumerate(copies)]
    for copy in running:
        copy.start()
    for copy in running:
        copy.wait()


def quads(ref, first, count=1):
    return ref.at[pl.ds(first * QUAD, count * QUAD)]


def pack_kernel(move_ref, owner_ref, own_out, other_out, slots_ref, used_ref, sems):
    slots_ref[...] = jnp.zeros(slots_ref.shape, slots_ref.dtype)
    for o in range(used_ref.shape[0]):
        used_ref[o] = 0
    me = lax.axis_index("kv")
    chip, core = me // 2, me % 2

    def place(p, carry):
        owner = owner_ref[p]
        rank = used_ref[owner]
        used_ref[owner] = rank + 1
        up = (owner // 2 - chip) & (CHIPS - 1)
        lands = owner % 2
        carrier = jnp.where(up == 0, lands, jnp.where(up == FAR, core, (up > FAR).astype(jnp.int32)))
        distance = jnp.where(up > FAR, CHIPS - up, up)
        slot = (distance - 1) * 4 + jnp.where(lands == carrier, 0, CAP)
        slot = jnp.where(up == 0, jnp.where(carrier == core, HOME, GIVEN), slot)
        slots_ref[jnp.where(carrier == core, slot, HOME + CAP + slot) + rank] = move_ref[p]
        return carry

    lax.fori_loop(0, move_ref.shape[0], place, 0, unroll=8)
    own, other = slots_ref.at[pl.ds(0, HOME + CAP)], slots_ref.at[pl.ds(HOME + CAP, GIVEN + CAP)]
    copy_all([(other, other_out), (own, own_out)], sems)


def short_copies(n, own_ref, got_ref, out_ref):
    copies = []
    for m in range(3):
        copies.append((quads(own_ref, n + 3 * m), quads(out_ref, 2 * m)))
        if n + 3 * m < FAR - 1:
            copies.append((quads(got_ref, n + 3 * m), quads(out_ref, 2 * m + 1)))
    return copies


def one_kernel(own_ref, got_ref, after_ref, out_ref, sems):
    del after_ref
    copy_all(short_copies(0, own_ref, got_ref, out_ref), sems)


def two_kernel(own_ref, got_ref, after_ref, out_ref, sems):
    del after_ref
    copy_all(short_copies(1, own_ref, got_ref, out_ref), sems)


def long_copies(first, own_ref, got_ref, one_ref, two_ref, out_ref):
    n = first // 3 - 1
    count = 2 - n
    return [
        (quads(own_ref, first - 1), quads(out_ref, 0)),
        (quads(got_ref, first - 1), quads(out_ref, 1)),
        (quads(one_ref, 2 + 2 * n, 2), quads(out_ref, 2, 2)),
        (quads(two_ref, 2 + 2 * n, count), quads(out_ref, 4, count)),
    ]


def three_kernel(own_ref, got_ref, one_ref, two_ref, out_ref, sems):
    copy_all(long_copies(3, own_ref, got_ref, one_ref, two_ref, out_ref), sems)


def six_kernel(own_ref, got_ref, one_ref, two_ref, after_ref, out_ref, sems):
    del after_ref
    copy_all(long_copies(6, own_ref, got_ref, one_ref, two_ref, out_ref), sems)


def arrived(one_ref, two_ref, three_ref, six_ref):
    return (
        (1, one_ref, 0),
        (2, two_ref, 0),
        (3, three_ref, 0),
        (4, three_ref, 2),
        (5, three_ref, 4),
        (6, six_ref, 0),
        (7, six_ref, 2),
    )


def give_kernel(one_ref, two_ref, three_ref, six_ref, after_ref, out_ref, sems):
    del after_ref
    core = lax.axis_index("kv") % 2
    page = out_ref.shape[1:]
    copies = [(six_ref.at[pl.ds(4 * QUAD + CAP, CAP)], out_ref.at[pl.ds(GIVEN, CAP)])]
    to = out_ref.at[pl.ds(0, GIVEN)].reshape((FAR - 1, 2, CAP) + page)
    for ref, distance, count in ((one_ref, 1, 1), (two_ref, 2, 1), (three_ref, 3, 3), (six_ref, 6, 2)):
        chunks = ref.at[pl.ds(0, 2 * QUAD * count)].reshape((count, 2, QUAD) + page)
        for other in range(2):
            start = core + other * (1 - 2 * core)
            source = chunks.at[:, other, pl.ds(CAP, CAP)]
            copies.append((source, to.at[pl.ds(distance - 1, count), start]))
    copy_all(copies, sems)


def rows(out_ref, up, start=0, count=CAP):
    chip = lax.axis_index("kv") // 2
    return out_ref.at[pl.ds(((chip + up) & (CHIPS - 1)) * QUAD + start * CAP, count)]


def land_kernel(own_ref, got_ref, one_ref, two_ref, three_ref, six_ref, out_ref, sems):
    core = lax.axis_index("kv") % 2
    way = 1 - 2 * core
    copies = [
        (own_ref.at[pl.ds(HOME, CAP)], rows(out_ref, 0, core)),
        (got_ref.at[pl.ds(GIVEN, CAP)], rows(out_ref, 0, 1 - core)),
        (six_ref.at[pl.ds(4 * QUAD, CAP)], rows(out_ref, FAR, core)),
    ]
    for distance, ref, quad in arrived(one_ref, two_ref, three_ref, six_ref):
        for quad, start in ((quad, core), (quad + 1, 1 - core)):
            copies.append((ref.at[pl.ds(quad * QUAD, CAP)], rows(out_ref, -way * distance, start)))
    copy_all(copies, sems)


def land_taken_kernel(taken_any, landed_ref, after_ref, out_ref, taken_ref, sems):
    del landed_ref, after_ref
    core = lax.axis_index("kv") % 2
    way = 1 - 2 * core
    pltpu.sync_copy(taken_any, taken_ref)
    copies = [(taken_ref.at[pl.ds(GIVEN, CAP)], rows(out_ref, FAR, 1 - core))]
    for distance in range(1, FAR):
        copies.append((quads(taken_ref, distance - 1), rows(out_ref, way * distance, 0, QUAD)))
    copy_all(copies, sems)


def combined(parts):
    shifts, values = parts[:, 8:, 0:1], parts[:, :8, :]
    sums = parts[:, 8:, 1:2] + parts[:, 8:, 4:5]
    shift = jnp.max(shifts, axis=0)
    factor = jnp.exp(shifts - shift[None])
    return shift, jnp.sum(sums * factor, axis=0), jnp.sum(values * factor, axis=0)


def fill_kernel(*refs):
    del refs


def column_kernel(parts_any, after_ref, out_ref, ids_ref, parts_ref):
    del after_ref
    pltpu.sync_copy(parts_any, parts_ref)
    parts = parts_ref[...].astype(F32)
    shift, weight_sum, values = combined(parts)
    lane = iota((8, HD), 1)
    extra = side_lanes(lane, shift, weight_sum)
    out = jnp.concatenate([values, extra], axis=0).astype(out_ref.dtype)
    out_ref[...] = jnp.broadcast_to(out[None], out_ref.shape)
    n = parts.shape[0]
    source, place = iota((n, n * CAP), 0), iota((n, n * CAP), 1)
    ids = parts[:, 8, :]
    ids = jnp.where(place % CAP == 0, ids[:, 2:3], ids[:, 3:4])
    ids_ref[...] = jnp.sum(jnp.where(source == place // CAP, ids, 0.0), axis=0, keepdims=True).astype(jnp.int32)


def project_kernel(parts_any, weight_ref, out_ref, parts_ref):
    pltpu.sync_copy(parts_any, parts_ref)
    _, weight_sum, values = combined(parts_ref[...].astype(F32))
    attended = (values / weight_sum).astype(BF16)
    upper = jnp.dot(attended, weight_ref[:HD], preferred_element_type=F32)
    lower = jnp.dot(attended, weight_ref[HD:], preferred_element_type=F32)
    out_ref[...] = upper[:B] + lower[B:]


def pair_kernel(parts_any, out_ref, parts_ref):
    pltpu.sync_copy(parts_any, parts_ref)
    both = (parts_ref[0] + parts_ref[1]).astype(out_ref.dtype)
    out_ref[...] = jnp.broadcast_to(both[None], out_ref.shape)


def add_kernel(parts_any, own_ref, out_ref, passed_ref, parts_ref):
    del own_ref, passed_ref
    pltpu.sync_copy(parts_any, parts_ref)
    out_ref[...] = jnp.sum(parts_ref[...].astype(F32), axis=0).astype(out_ref.dtype)


def local(queries, res_cache, res_count, move_cache, move_request, move_owner, out_weight):
    kv_size, tp_size = lax.axis_size("kv"), lax.axis_size("tp")
    owners = move_owner.reshape(-1)
    page = move_cache.shape[1:]

    def pages(n):
        return jax.ShapeDtypeStruct((n,) + page, BF16)

    def shift(x, chips):
        pairs = [(i, (i + 2 * chips * (1 - 2 * (i % 2))) % kv_size) for i in range(kv_size)]
        return lax.ppermute(x, "kv", pairs)

    def swap(x):
        return lax.ppermute(x, "kv", [(i, i ^ 1) for i in range(kv_size)])

    own, other = pl.pallas_call(
        pack_kernel,
        out_shape=(pages(HOME + CAP), pages(GIVEN + CAP)),
        in_specs=[VMEM, SMEM],
        out_specs=(ANY, ANY),
        scratch_shapes=[
            pltpu.VMEM((HOME + GIVEN + 2 * CAP,) + page, BF16),
            pltpu.SMEM((kv_size,), jnp.int32),
            pltpu.SemaphoreType.DMA((2,)),
        ],
        compiler_params=pltpu.CompilerParams(vmem_limit_bytes=LARGE),
        name="pack",
    )(move_cache, owners)
    got = swap(other)
    def copies(kernel, name, out_pages, count, *args):
        return pl.pallas_call(
            kernel,
            out_shape=tuple(pages(n) for n in out_pages),
            in_specs=[ANY] * len(args),
            out_specs=(ANY,) * len(out_pages),
            scratch_shapes=[pltpu.SemaphoreType.DMA((count,))],
            compiler_params=pltpu.CompilerParams(vmem_limit_bytes=SMALL),
            cost_estimate=pl.CostEstimate(flops=0, bytes_accessed=1024, transcendentals=0),
            name=name,
        )(*args)

    parts = pl.pallas_call(
        attend_kernel,
        out_shape=jax.ShapeDtypeStruct((kv_size, 16, HD), BF16),
        in_specs=[VMEM, VMEM, VMEM, SMEM, SMEM, VMEM, VMEM],
        out_specs=VMEM,
        name="attend",
    )(queries, res_cache, move_cache, res_count, move_request, owners[None, :], move_request[None, :])
    (one,) = copies(one_kernel, "one", (6 * QUAD,), 6, own, got, parts)
    (two,) = copies(two_kernel, "two", (5 * QUAD,), 5, own, got, one)
    one, two = shift(one, 1), shift(two, 2)
    parts = lax.all_to_all(parts, "kv", split_axis=0, concat_axis=0, tiled=True)
    (three,) = copies(three_kernel, "three", (6 * QUAD,), 4, own, got, one, two)
    (six,) = copies(six_kernel, "six", (5 * QUAD,), 4, own, got, one, two, three)
    six_up, three_up = shift(six, 6), shift(three, 3)
    own = pl.pallas_call(
        fill_kernel,
        out_shape=pages(HOME + CAP),
        in_specs=[ANY],
        out_specs=ANY,
        input_output_aliases={0: 0},
        compiler_params=pltpu.CompilerParams(vmem_limit_bytes=SMALL),
        cost_estimate=pl.CostEstimate(flops=10**11, bytes_accessed=1024, transcendentals=0),
        name="fill",
    )(own)
    part, landed_ids = pl.pallas_call(
        column_kernel,
        out_shape=(
            jax.ShapeDtypeStruct((tp_size, 16, HD), BF16),
            jax.ShapeDtypeStruct((1, kv_size * CAP), jnp.int32),
        ),
        in_specs=[ANY, ANY],
        out_specs=(VMEM, VMEM),
        scratch_shapes=[pltpu.VMEM(parts.shape, BF16)],
        compiler_params=pltpu.CompilerParams(vmem_limit_bytes=SMALL),
        name="column",
        cost_estimate=pl.CostEstimate(flops=0, bytes_accessed=1024, transcendentals=0),
    )(parts, own)
    six, three = six_up, three_up
    columns = lax.all_to_all(part, "tp", split_axis=0, concat_axis=0, tiled=True)
    partial_out = pl.pallas_call(
        project_kernel,
        out_shape=jax.ShapeDtypeStruct((B, out_weight.shape[1]), F32),
        in_specs=[ANY, VMEM],
        out_specs=VMEM,
        scratch_shapes=[pltpu.VMEM(columns.shape, BF16)],
        compiler_params=pltpu.CompilerParams(vmem_limit_bytes=SMALL),
        name="project",
    )(columns, out_weight)
    pair = lax.all_gather(
        partial_out, "kv", axis_index_groups=[[2 * z, 2 * z + 1] for z in range(CHIPS)]
    )
    chip_out = pl.pallas_call(
        pair_kernel,
        out_shape=jax.ShapeDtypeStruct((CHIPS, B, out_weight.shape[1]), BF16),
        in_specs=[ANY],
        out_specs=VMEM,
        scratch_shapes=[pltpu.VMEM(pair.shape, F32)],
        compiler_params=pltpu.CompilerParams(vmem_limit_bytes=SMALL),
        name="pair",
    )(pair)
    partials = lax.all_to_all(
        chip_out,
        "kv",
        split_axis=0,
        concat_axis=0,
        tiled=True,
        axis_index_groups=[[2 * z + c for z in range(CHIPS)] for c in range(2)],
    )
    (give,) = copies(give_kernel, "give", (GIVEN + CAP,), 9, one, two, three, six, chip_out)
    taken = swap(give)
    (landed,) = copies(land_kernel, "land", (kv_size * CAP,), 17, own, got, one, two, three, six)
    mixed, own = pl.pallas_call(
        add_kernel,
        out_shape=(jax.ShapeDtypeStruct((B, out_weight.shape[1]), BF16), pages(HOME + CAP)),
        in_specs=[ANY, ANY],
        out_specs=(VMEM, ANY),
        input_output_aliases={1: 1},
        scratch_shapes=[pltpu.VMEM(partials.shape, BF16)],
        compiler_params=pltpu.CompilerParams(vmem_limit_bytes=SMALL),
        name="add",
    )(partials, own)
    landed = pl.pallas_call(
        land_taken_kernel,
        out_shape=pages(kv_size * CAP),
        in_specs=[ANY] * 3,
        out_specs=ANY,
        input_output_aliases={1: 0},
        scratch_shapes=[pltpu.VMEM(taken.shape, BF16), pltpu.SemaphoreType.DMA((FAR,))],
        compiler_params=pltpu.CompilerParams(vmem_limit_bytes=SMALL),
        cost_estimate=pl.CostEstimate(flops=0, bytes_accessed=1024, transcendentals=0),
        name="land_taken",
    )(taken, landed, own)
    return (mixed, landed, landed_ids.reshape(-1))


def solution(mesh):
    placed = (
        P(),
        P(("kv", "tp"), None, None, None),
        P(("kv", "tp"), None),
        P(("kv", "tp"), None, None, None),
        P(("kv", "tp")),
        P(("kv", "tp"), None),
        P("kv", "tp"),
    )
    return jax.shard_map(
        local,
        mesh=mesh,
        in_specs=placed,
        out_specs=(P(None, "tp"), P(("kv", "tp"), None, None, None), P(("kv", "tp"))),
        check_vma=False,
    )
```
